32 devices in a mesh: ctx: 8 (over z, x), tp: 4 (over y, core).
Axes of the slice: x: 2, y: 2, z: 4, core: 2. Of those that a mesh axis runs over, the one named last changes fastest.
Arguments:
- tokens: bfloat16 [4, 512, 2048], P(None, 'ctx'), may hold values from -6 to 6
- cotangent: bfloat16 [4, 512, 2048], P(None, 'ctx'), may hold values from -6 to 6
- routes: int32 [4, 512, 8], P(None, 'ctx'), may hold values from 0 to 15, all different within a row; in each aligned block of 64 rows (0 to 63, 64 to 127, ..., all dimensions but the last counted through in order) at most 48 rows name the same one
- attn_gain: bfloat16 [2048], P('ctx'), may hold values from 0.099609375 to 1.8984375
- ffn_gain: bfloat16 [2048], P('ctx'), may hold values from 0.099609375 to 1.8984375
- qk_gain: bfloat16 [128, 2], P('ctx'), may hold values from 0.099609375 to 1.8984375
- w_query: bfloat16 [2048, 2048], P('ctx', 'tp'), may hold values from -0.125 to 0.125
- w_key: bfloat16 [2048, 2048], P('ctx', 'tp'), may hold values from -0.125 to 0.125
- w_value: bfloat16 [2048, 2048], P('ctx', 'tp'), may hold values from -0.125 to 0.125
- w_out: bfloat16 [2048, 2048], P('ctx', 'tp'), may hold values from -1.5 to 1.5
- router: bfloat16 [2048, 16], P('ctx'), may hold values from -0.0625 to 0.0625
- w_gate: bfloat16 [16, 2048, 1024], P(None, 'ctx', 'tp'), may hold values from -0.125 to 0.125
- w_up: bfloat16 [16, 2048, 1024], P(None, 'ctx', 'tp'), may hold values from -0.125 to 0.125
- w_down: bfloat16 [16, 2048, 1024], P(None, 'ctx', 'tp'), may hold values from -1.5 to 1.5
Outputs:
- layer_out: bfloat16 [4, 512, 2048], P(None, 'ctx')
- input_grad: bfloat16 [4, 512, 2048], P(None, 'ctx')
- grad_attn_gain: float32 [2048], P('ctx')
- grad_ffn_gain: float32 [2048], P('ctx')
- grad_qk_gain: float32 [128, 2], P('ctx')
- grad_query: float32 [2048, 2048], P('ctx', 'tp')
- grad_key: float32 [2048, 2048], P('ctx', 'tp')
- grad_value: float32 [2048, 2048], P('ctx', 'tp')
- grad_out: float32 [2048, 2048], P('ctx', 'tp')
- grad_router: float32 [2048, 16], P('ctx')
- grad_gate: float32 [16, 2048, 1024], P(None, 'ctx', 'tp')
- grad_up: float32 [16, 2048, 1024], P(None, 'ctx', 'tp')
- grad_down: float32 [16, 2048, 1024], P(None, 'ctx', 'tp')
The draws below stay inside these ranges and needn't reach their ends.
Inputs may be any that keep to these rules, and one draw needn't show every extreme that they name: `routes`: A token names 8 different experts. Among the 64 tokens of one sequence that one device holds, no expert is named more than 48 times, and in some such block one expert is named exactly 48 times.
All inputs are finite; a program needn't handle non-finite values.
Results may differ from the reference program's by a relative error of at most 0.024.
Values may be sent and summed in bfloat16 or wider, within the bound.
A program may use at most 320 MiB of HBM per device.

```python
import math
import jax
import jax.numpy as jnp
import numpy as np
from jax import lax

D = 2048
H = 16
HD = 128
FF = 1024
TOPK = 8
E = 16
SL_DEV = 64
SEQS = 4
MOST = 48
LEN = 512


def shard_levels(key, extent, cuts, least, largest):
    factor_of, own = 1.0, jax.random.fold_in(key, 6)
    for position, parts in cuts:
        steps = jnp.exp(jax.random.uniform(jax.random.fold_in(own, position), (parts,), jnp.float32, least / len(cuts), largest / len(cuts)))
        factor_of = factor_of * jnp.repeat(steps, extent[position] // parts).reshape([-1 if axis == position else 1 for axis in range(len(extent))])
    return factor_of


def deal_out(rng, own, number, rows, amount, top, bound, slope):
    ranking = jax.random.permutation(rng, amount)
    crowded, common = portions_of(amount, rows * top, bound, slope, True), portions_of(amount, rows * top, bound, slope, False)
    places = jnp.arange(amount)

    def named(lengths, rotation):
        used = int((lengths > 0).sum())
        fixed = max(1, used // 4)
        passed = fixed + (places - fixed + rotation * (used - fixed)) % max(1, amount - fixed)
        return jnp.zeros((amount,), jnp.int32).at[ranking[jnp.where(places < fixed, places, passed)]].set(jnp.asarray(lengths, jnp.int32))

    lengths = jnp.where(number % 4 == 0, named(crowded, number // 4), named(common, number - number // 4 - 1))
    mixed = jax.random.permutation(jax.random.fold_in(own, 3), amount)
    source_of, sink = mixed[0:amount // 2 * 2:2], mixed[1:amount // 2 * 2:2]
    margin = jnp.minimum(lengths[source_of] - 1, bound - lengths[sink]) // 2
    margin = jnp.where((source_of == ranking[0]) | (sink == ranking[0]) | (lengths[sink] == 0), 0, jnp.maximum(margin, 0))
    passed = jax.random.randint(jax.random.fold_in(own, 4), (amount // 2,), 0, 1 << 20) % (margin + 1)
    lengths = lengths.at[source_of].add(-passed).at[sink].add(passed)
    members = jnp.searchsorted(jnp.cumsum(lengths), jnp.arange(rows * top), side="right").astype(jnp.int32)
    grid = members.reshape(top, rows).T
    grid = grid[jax.random.permutation(jax.random.fold_in(own, 1), rows)]
    rotation = jax.random.randint(jax.random.fold_in(own, 2), (rows, 1), 0, top)
    return jnp.take_along_axis(grid, (jnp.arange(top)[None, :] + rotation) % top, axis=1)


def portions_of(number_of, total, most, skew, full):
    loads = [(1 << 20) // math.isqrt(grade ** skew) + 1 for grade in range(1, number_of + 1)]
    largest = most if full else min(most, max(-(-total // number_of), total * loads[0] // sum(loads)))
    least = 1 if total - largest >= number_of - 1 else 0
    counts, rest = [largest] + [least] * (number_of - 1), total - largest - least * (number_of - 1)
    while rest > 0:
        movable = [i for i in range(1, number_of) if counts[i] < largest] or [i for i in range(1, number_of) if counts[i] < most]
        pool, remaining = sum([loads[i] for i in movable]), rest
        for i in movable:
            addition = min(most - counts[i], max(1, remaining * loads[i] // pool), rest)
            counts[i] = counts[i] + addition
            rest = rest - addition
    return np.array(counts)


def gaussian(own_key, shape, width, limit, shards=(), held_as=jnp.bfloat16):
    values = jax.random.normal(own_key, shape, jnp.float32) * width
    if len(shards) > 0:
        values = shard_levels(own_key, shape, shards, -0.22, 0.18) * values
    return jnp.clip(values, min=-limit, max=limit).astype(held_as)


def setup_inputs(seed: int = 0) -> dict:
    key_list = jax.random.split(jax.random.key(seed), 15)
    tokens = gaussian(key_list[0], (SEQS, LEN, D), 1.0, 6.0, ((1, 8),))
    cotangent = gaussian(key_list[1], (SEQS, LEN, D), 1.0, 6.0, ((1, 8),))
    routes_keys = jax.random.split(jax.random.fold_in(key_list[2], 1), SEQS * LEN // SL_DEV)
    routes_turns = jax.random.permutation(jax.random.fold_in(key_list[2], 3), SEQS * LEN // SL_DEV)
    routes = jax.vmap(lambda own, number: deal_out(jax.random.fold_in(key_list[2], 2), own, number, SL_DEV, E, TOPK, MOST, 2))(routes_keys, routes_turns).reshape((SEQS, LEN, TOPK))
    attn_gain = jnp.clip(1.0 + 0.18 * jax.random.normal(key_list[3], (D,), jnp.float32), 0.099609375, 1.8984375).astype(jnp.bfloat16)
    ffn_gain = jnp.clip(1.0 + 0.18 * jax.random.normal(key_list[4], (D,), jnp.float32), 0.099609375, 1.8984375).astype(jnp.bfloat16)
    qk_gain = jnp.clip(1.0 + 0.18 * jax.random.normal(key_list[5], (HD, 2), jnp.float32), 0.099609375, 1.8984375).astype(jnp.bfloat16)
    w_query = gaussian(key_list[6], (D, H * HD), D ** -0.5, 0.125, ((0, 8), (1, 4)))
    w_key = gaussian(key_list[7], (D, H * HD), D ** -0.5, 0.125, ((0, 8), (1, 4)))
    w_value = gaussian(key_list[8], (D, H * HD), D ** -0.5, 0.125, ((0, 8), (1, 4)))
    w_out = gaussian(key_list[9], (D, H * HD), (max(1, 4 * H * HD // LEN)) ** -0.5, 1.5, ((0, 8), (1, 4)))
    router = gaussian(key_list[10], (D, E), (4 * D) ** -0.5, 0.0625, ((0, 8),))
    w_gate = gaussian(key_list[11], (E, D, FF), D ** -0.5, 0.125, ((1, 8), (2, 4)))
    w_up = gaussian(key_list[12], (E, D, FF), D ** -0.5, 0.125, ((1, 8), (2, 4)))
    w_down = gaussian(key_list[13], (E, D, FF), (max(1, FF // 64)) ** -0.5, 1.5, ((1, 8), (2, 4)))
    return {"tokens": tokens, "cotangent": cotangent, "routes": routes, "attn_gain": attn_gain, "ffn_gain": ffn_gain, "qk_gain": qk_gain, "w_query": w_query, "w_key": w_key, "w_value": w_value, "w_out": w_out, "router": router, "w_gate": w_gate, "w_up": w_up, "w_down": w_down}


EPS = 1e-06
ROPE_BASE = 50000.0

@jax.custom_vjp
def low(v):
    return lax.optimization_barrier(v.astype(jnp.bfloat16)).astype(jnp.float32)

@jax.custom_vjp
def low_back(v):
    return v

def low_keep(v):
    return (low(v), None)

def low_pass(kept, grad):
    return (grad,)

def back_keep(v):
    return (v, None)

def back_low(kept, grad):
    return (low(grad),)
low.defvjp(low_keep, low_pass)
low_back.defvjp(back_keep, back_low)

def matmul_high(left_op, right_op):
    return jnp.dot(left_op, right_op, precision=lax.Precision.HIGHEST)

def rms_norm(values, gain_vec):
    return values * lax.rsqrt(lax.optimization_barrier(jnp.mean(values * values, axis=-1, keepdims=True)) + EPS) * gain_vec

def rotate(values, cosines, sines):
    half_size = values.shape[-1] // 2
    first_half = values[..., :half_size]
    second_half = values[..., half_size:]
    return jnp.concatenate([first_half * cosines - second_half * sines, second_half * cosines + first_half * sines], axis=-1)

def rope_tables(seq_len):
    positions = jnp.arange(seq_len).astype(jnp.float32)
    frequencies = ROPE_BASE ** (-2.0 * jnp.arange(HD // 2).astype(jnp.float32) / HD)
    angles = positions[:, None] * frequencies[None, :]
    return (jnp.cos(angles)[:, None, :], jnp.sin(angles)[:, None, :])

def attend(query, keys, values):
    seq_len = query.shape[0]
    block_rows = min(512, seq_len)

    def one_block(block_query):
        scores = low_back(jnp.einsum('qhd,khd->hqk', block_query, keys, precision=lax.Precision.HIGHEST))
        exponent = jnp.exp(scores)
        denominator = lax.optimization_barrier(jnp.sum(exponent, axis=-1))
        accum_sum = low_back(jnp.einsum('hqk,khd->qhd', low(exponent), values, precision=lax.Precision.HIGHEST))
        return accum_sum / jnp.transpose(denominator)[:, :, None]
    blocks = query.reshape(seq_len // block_rows, block_rows, H, HD)
    return lax.map(jax.checkpoint(one_block), blocks).reshape(seq_len, H, HD)

def layer(inputs, attn_gain, ffn_gain, qk_gain, w_query, w_key, w_value, w_out, router, w_gate, w_up, w_down, route_rows):
    seq_len = inputs.shape[0]
    normed = low(rms_norm(inputs, attn_gain))
    query_lin = low_back(matmul_high(normed, w_query)).reshape(seq_len, H, HD)
    key_lin = low_back(matmul_high(normed, w_key)).reshape(seq_len, H, HD)
    value_rows = low(low_back(matmul_high(normed, w_value))).reshape(seq_len, H, HD)
    cosines, sines = rope_tables(seq_len)
    query = low(rotate(rms_norm(query_lin, qk_gain[:, 0]), cosines, sines) * HD ** (-0.5))
    keys = low(rotate(rms_norm(key_lin, qk_gain[:, 1]), cosines, sines))
    attended = attend(query, keys, value_rows).reshape(seq_len, H * HD)
    branch = low_back(matmul_high(low(attended), w_out.T))
    middle = inputs + branch
    normed_ffn = low(rms_norm(middle, ffn_gain))
    logits = low_back(matmul_high(normed_ffn, router))
    probs = jax.nn.softmax(logits, axis=-1)
    chosen = lax.optimization_barrier(jnp.sum((route_rows[:, :, None] == jnp.arange(E)[None, None, :]).astype(jnp.float32), axis=1))
    gates = probs * chosen

    def one_expert(total, packed):
        gate_w, up_w, down_w, gate_col = packed
        gate_pre = low_back(matmul_high(normed_ffn, gate_w))
        up_pre = low_back(matmul_high(normed_ffn, up_w))
        hidden = low(gate_col[:, None] * (jax.nn.silu(gate_pre) * up_pre))
        return (total + matmul_high(hidden, down_w.T), None)
    mixed, unused = lax.scan(jax.checkpoint(one_expert), jnp.zeros_like(middle), (w_gate, w_up, w_down, gates.T))
    return middle + low_back(mixed)

def reference(tokens, cotangent, routes, attn_gain, ffn_gain, qk_gain, w_query, w_key, w_value, w_out, router, w_gate, w_up, w_down):
    weights = tuple((item.astype(jnp.float32) for item in (attn_gain, ffn_gain, qk_gain, w_query, w_key, w_value, w_out, router, w_gate, w_up, w_down)))

    def one_sequence(sums, packed):
        seq_tokens, seq_cot, seq_routes = packed

        def forward(inputs, p_attn, p_ffn, p_qk, p_query, p_key, p_value, p_out, p_router, p_gate, p_up, p_down):
            return layer(inputs, p_attn, p_ffn, p_qk, p_query, p_key, p_value, p_out, p_router, p_gate, p_up, p_down, seq_routes)
        result, pull = jax.vjp(forward, seq_tokens.astype(jnp.float32), weights[0], weights[1], weights[2], weights[3], weights[4], weights[5], weights[6], weights[7], weights[8], weights[9], weights[10])
        grads = pull(seq_cot.astype(jnp.float32))
        sums = tuple((total + part for total, part in zip(sums, grads[1:])))
        return (sums, (result.astype(jnp.bfloat16), grads[0].astype(jnp.bfloat16)))
    initial = tuple((jnp.zeros_like(item) for item in weights))
    sums, outputs = lax.scan(one_sequence, initial, (tokens, cotangent, routes))
    return (outputs[0], outputs[1], sums[0], sums[1], sums[2], sums[3], sums[4], sums[5], sums[6], sums[7], sums[8], sums[9], sums[10])
```

```python
import jax
import jax.numpy as jnp
from jax import lax
from jax.sharding import PartitionSpec as P

MICRO = 2
MOST = 48


EPS = 1e-06
ROPE_BASE = 50000.0


def product(left_op, right_op):
    return jnp.dot(left_op, right_op, preferred_element_type=jnp.float32)


def rotate(values, cosines, sines):
    half_size = values.shape[-1] // 2
    first_half = values[..., :half_size]
    second_half = values[..., half_size:]
    return jnp.concatenate(
        [first_half * cosines - second_half * sines, second_half * cosines + first_half * sines],
        axis=-1,
    )


def inverse_rms(values):
    return lax.rsqrt(jnp.mean(values * values, axis=-1, keepdims=True) + EPS)


def norm_back(gradient, inputs, scaling, gain_vec):
    weighted = gradient * gain_vec
    return scaling * weighted - inputs * scaling**3 * jnp.mean(
        weighted * inputs, axis=-1, keepdims=True
    )


def fetch_dense(attn_gain, ffn_gain, qk_gain, w_query, w_key, w_value, w_out, router):
    return (
        lax.all_gather(attn_gain, "ctx", axis=0, tiled=True),
        lax.all_gather(ffn_gain, "ctx", axis=0, tiled=True),
        lax.all_gather(qk_gain, "ctx", axis=0, tiled=True),
        lax.all_gather(w_query, "ctx", axis=0, tiled=True),
        lax.all_gather(w_key, "ctx", axis=0, tiled=True),
        lax.all_gather(w_value, "ctx", axis=0, tiled=True),
        lax.all_gather(w_out, "ctx", axis=0, tiled=True),
        lax.all_gather(router, "ctx", axis=0, tiled=True),
    )


def fetch_experts(w_gate, w_up, w_down):
    return (
        lax.all_gather(w_gate, "ctx", axis=1, tiled=True),
        lax.all_gather(w_up, "ctx", axis=1, tiled=True),
        lax.all_gather(w_down, "ctx", axis=1, tiled=True),
    )


def reduce_grads(dense_grads, expert_grads):
    dense_owned = (
        lax.psum_scatter(
            dense_grads[0].astype(jnp.bfloat16), "ctx", scatter_dimension=0, tiled=True
        ).astype(jnp.float32),
        lax.psum_scatter(
            dense_grads[1].astype(jnp.bfloat16), "ctx", scatter_dimension=0, tiled=True
        ).astype(jnp.float32),
        lax.psum_scatter(
            dense_grads[2].astype(jnp.bfloat16), "ctx", scatter_dimension=0, tiled=True
        ).astype(jnp.float32),
        lax.psum_scatter(
            dense_grads[3].astype(jnp.bfloat16), "ctx", scatter_dimension=0, tiled=True
        ).astype(jnp.float32),
        lax.psum_scatter(
            dense_grads[4].astype(jnp.bfloat16), "ctx", scatter_dimension=0, tiled=True
        ).astype(jnp.float32),
        lax.psum_scatter(
            dense_grads[5].astype(jnp.bfloat16), "ctx", scatter_dimension=0, tiled=True
        ).astype(jnp.float32),
        lax.psum_scatter(
            dense_grads[6].astype(jnp.bfloat16), "ctx", scatter_dimension=0, tiled=True
        ).astype(jnp.float32),
        lax.psum_scatter(
            dense_grads[7].astype(jnp.bfloat16), "ctx", scatter_dimension=0, tiled=True
        ).astype(jnp.float32),
    )
    expert_owned = (
        lax.psum_scatter(
            expert_grads[0].astype(jnp.bfloat16), "ctx", scatter_dimension=1, tiled=True
        ).astype(jnp.float32),
        lax.psum_scatter(
            expert_grads[1].astype(jnp.bfloat16), "ctx", scatter_dimension=1, tiled=True
        ).astype(jnp.float32),
        lax.psum_scatter(
            expert_grads[2].astype(jnp.bfloat16), "ctx", scatter_dimension=1, tiled=True
        ).astype(jnp.float32),
    )
    return (tuple(dense_owned), tuple(expert_owned))


def add_all(earlier, latest):
    if earlier is None:
        return latest
    return tuple((first_one + second_one for first_one, second_one in zip(earlier, latest)))


def attend_forward(query, key_rows, value_rows):
    batch_count, query_count, head_count, head_size = query.shape

    def add_piece(state_pair, pieces, offset):
        key_piece = pieces[0].reshape(batch_count, -1, head_count, head_size)
        value_piece = pieces[1].reshape(batch_count, -1, head_count, head_size)
        scores = jnp.einsum("bqhd,bkhd->bhqk", query, key_piece, preferred_element_type=jnp.float32)
        exponent = jnp.exp(scores)
        denominator = jnp.sum(exponent, axis=-1)
        accum_sum = jnp.einsum(
            "bhqk,bkhd->bqhd",
            exponent.astype(jnp.bfloat16),
            value_piece,
            preferred_element_type=jnp.float32,
        )
        return (accum_sum, denominator)

    initial = (
        jnp.zeros(query.shape, jnp.float32),
        jnp.zeros((batch_count, head_count, query_count), jnp.float32),
    )
    return add_piece(
        initial,
        (
            lax.all_gather(key_rows, "ctx", axis=1, tiled=True),
            lax.all_gather(value_rows, "ctx", axis=1, tiled=True),
        ),
        jnp.int32(0),
    )


def attend_backward(query, key_rows, value_rows, grad_acc, grad_total):
    batch_count, query_count, head_count, head_size = query.shape
    full_len = key_rows.shape[1] * lax.axis_size("ctx")

    def add_piece(state_three, pieces, offset):
        key_piece = pieces[0].reshape(batch_count, -1, head_count, head_size)
        value_piece = pieces[1].reshape(batch_count, -1, head_count, head_size)
        piece_len = key_piece.shape[1]
        scores = jnp.einsum("bqhd,bkhd->bhqk", query, key_piece, preferred_element_type=jnp.float32)
        exponent = jnp.exp(scores)
        grad_prob = jnp.einsum(
            "bqhd,bkhd->bhqk", grad_acc, value_piece, preferred_element_type=jnp.float32
        )
        grad_score = (exponent * (grad_prob + grad_total[..., None])).astype(jnp.bfloat16)
        grad_query = jnp.einsum(
            "bhqk,bkhd->bqhd", grad_score, key_piece, preferred_element_type=jnp.float32
        )
        key_term = jnp.einsum(
            "bhqk,bqhd->bkhd", grad_score, query, preferred_element_type=jnp.float32
        ).reshape(batch_count, piece_len, -1)
        value_term = jnp.einsum(
            "bhqk,bqhd->bkhd",
            exponent.astype(jnp.bfloat16),
            grad_acc,
            preferred_element_type=jnp.float32,
        ).reshape(batch_count, piece_len, -1)
        return (grad_query, key_term, value_term)

    initial = (jnp.zeros(query.shape, jnp.float32),)
    initial = initial + (
        jnp.zeros((batch_count, full_len, head_count * head_size), jnp.float32),
        jnp.zeros((batch_count, full_len, head_count * head_size), jnp.float32),
    )
    return add_piece(
        initial,
        (
            lax.all_gather(key_rows, "ctx", axis=1, tiled=True),
            lax.all_gather(value_rows, "ctx", axis=1, tiled=True),
        ),
        jnp.int32(0),
    )


def dispatch(route_block, gate_item, expert_count):
    group_count, local_len, chosen_count = route_block.shape
    expert_ids = route_block.reshape(group_count, local_len * chosen_count)
    onehot = (expert_ids[..., None] == jnp.arange(expert_count)[None, None, :]).astype(jnp.int32)
    before = jnp.cumsum(onehot, axis=1) - onehot
    position = jnp.sum(before * onehot, axis=2)
    slot_index = (
        expert_ids * (group_count * MOST) + jnp.arange(group_count)[:, None] * MOST + position
    )
    owner_row = (
        jnp.arange(group_count)[:, None] * local_len
        + jnp.arange(local_len * chosen_count)[None, :] // chosen_count
    )
    slot_index = slot_index.reshape(-1)
    source_rows = (
        jnp.zeros(expert_count * group_count * MOST, jnp.int32)
        .at[slot_index]
        .set(owner_row.reshape(-1))
    )
    gate_slot = (
        jnp.zeros(expert_count * group_count * MOST, jnp.float32)
        .at[slot_index]
        .set(gate_item.reshape(-1))
    )
    return (slot_index, source_rows, gate_slot)


def per_device(
    tokens,
    cotangent,
    routes,
    attn_gain,
    ffn_gain,
    qk_gain,
    w_query,
    w_key,
    w_value,
    w_out,
    router,
    w_gate,
    w_up,
    w_down,
):
    sequences, local_len, model_width = tokens.shape
    head_size = qk_gain.shape[0] * lax.axis_size("ctx")
    head_count = w_query.shape[1] // head_size
    expert_count = w_gate.shape[0]
    chosen_count = routes.shape[2]
    group_count = sequences // MICRO
    row_count = group_count * local_len
    half_size = head_size // 2
    positions = (lax.axis_index("ctx") * local_len + jnp.arange(local_len)).astype(jnp.float32)
    frequencies = ROPE_BASE ** (-2.0 * jnp.arange(half_size).astype(jnp.float32) / head_size)
    angles = positions[:, None] * frequencies[None, :]
    cosines = jnp.cos(angles)[None, :, None, :]
    sines = jnp.sin(angles)[None, :, None, :]
    score_scale = head_size ** (-0.5)
    shape_heads = (group_count, local_len, head_count, head_size)
    dense_total = None
    expert_total = None
    out_parts = []
    grad_parts = []
    for micro_step in range(MICRO):
        first_seq = micro_step * group_count
        inputs = (
            tokens[first_seq : first_seq + group_count]
            .astype(jnp.float32)
            .reshape(row_count, model_width)
        )
        route_block = routes[first_seq : first_seq + group_count]
        upstream = (
            cotangent[first_seq : first_seq + group_count]
            .astype(jnp.float32)
            .reshape(row_count, model_width)
        )
        gain_attn, gain_ffn, gain_qk, full_query, full_key, full_value, full_out, full_router = (
            fetch_dense(attn_gain, ffn_gain, qk_gain, w_query, w_key, w_value, w_out, router)
        )
        full_gate, full_up, full_down = fetch_experts(w_gate, w_up, w_down)
        attn_vec = gain_attn.astype(jnp.float32)
        ffn_vec = gain_ffn.astype(jnp.float32)
        query_gain = gain_qk[:, 0].astype(jnp.float32)
        key_gain = gain_qk[:, 1].astype(jnp.float32)
        scale_one = inverse_rms(inputs)
        normed = (inputs * scale_one * attn_vec).astype(jnp.bfloat16)
        query_lin = product(normed, full_query).reshape(shape_heads)
        key_lin = product(normed, full_key).reshape(shape_heads)
        value_send = (
            product(normed, full_value).astype(jnp.bfloat16).reshape(group_count, local_len, -1)
        )
        query_scale = inverse_rms(query_lin)
        key_scale = inverse_rms(key_lin)
        query_hat = query_lin * query_scale
        key_hat = key_lin * key_scale
        query = (rotate(query_hat * query_gain, cosines, sines) * score_scale).astype(jnp.bfloat16)
        key_rows = (
            rotate(key_hat * key_gain, cosines, sines)
            .astype(jnp.bfloat16)
            .reshape(group_count, local_len, -1)
        )
        accum_sum, denominator = attend_forward(query, key_rows, value_send)
        per_row_total = jnp.transpose(denominator, (0, 2, 1))[..., None]
        attended = accum_sum / per_row_total
        attended_low = attended.astype(jnp.bfloat16).reshape(row_count, -1)
        branch = lax.psum(
            jnp.einsum("nc,dc->nd", attended_low, full_out, preferred_element_type=jnp.float32),
            "tp",
        )
        middle = inputs + branch
        scale_two = inverse_rms(middle)
        normed_ffn = (middle * scale_two * ffn_vec).astype(jnp.bfloat16)
        logits = product(normed_ffn, full_router)
        probs = jax.nn.softmax(logits, axis=-1)
        route_flat = route_block.reshape(row_count, chosen_count)
        picked = (route_flat[:, :, None] == jnp.arange(expert_count)[None, None, :]).astype(
            jnp.float32
        )
        gate_item = jnp.sum(picked * probs[:, None, :], axis=-1)
        slot_index, source_rows, gate_slot = dispatch(route_block, gate_item, expert_count)
        expert_in = normed_ffn[source_rows].reshape(expert_count, -1, model_width)
        gate_pre = jnp.einsum(
            "erd,edf->erf", expert_in, full_gate, preferred_element_type=jnp.float32
        )
        up_pre = jnp.einsum("erd,edf->erf", expert_in, full_up, preferred_element_type=jnp.float32)
        activated = jax.nn.silu(gate_pre) * up_pre
        gate_col = gate_slot.reshape(expert_count, -1)[:, :, None]
        hidden = (gate_col * activated).astype(jnp.bfloat16)
        expert_out = jnp.einsum(
            "erf,edf->erd", hidden, full_down, preferred_element_type=jnp.float32
        )
        mixed_part = (
            jnp.zeros((row_count, model_width), jnp.float32)
            .at[source_rows]
            .add(expert_out.reshape(-1, model_width))
        )
        mixed = lax.psum(mixed_part.astype(jnp.bfloat16), "tp").astype(jnp.float32)
        out_parts.append(
            (middle + mixed).astype(jnp.bfloat16).reshape(group_count, local_len, model_width)
        )
        gain_attn, gain_ffn, gain_qk, full_query, full_key, full_value, full_out, full_router = (
            fetch_dense(attn_gain, ffn_gain, qk_gain, w_query, w_key, w_value, w_out, router)
        )
        full_gate, full_up, full_down = fetch_experts(w_gate, w_up, w_down)
        grad_mixed = upstream.astype(jnp.bfloat16)
        grad_rows = grad_mixed[source_rows].reshape(expert_count, -1, model_width)
        grad_down_w = jnp.einsum(
            "erd,erf->edf", grad_rows, hidden, preferred_element_type=jnp.float32
        )
        grad_hidden = jnp.einsum(
            "erd,edf->erf", grad_rows, full_down, preferred_element_type=jnp.float32
        )
        gate_slot_grad = jnp.sum(grad_hidden * activated, axis=-1)
        grad_act = gate_col * grad_hidden
        sigmoid_gate = jax.nn.sigmoid(gate_pre)
        grad_up_pre = (grad_act * jax.nn.silu(gate_pre)).astype(jnp.bfloat16)
        grad_gate_pre = (
            grad_act * up_pre * sigmoid_gate * (1.0 + gate_pre * (1.0 - sigmoid_gate))
        ).astype(jnp.bfloat16)
        grad_gate_w = jnp.einsum(
            "erd,erf->edf", expert_in, grad_gate_pre, preferred_element_type=jnp.float32
        )
        grad_up_w = jnp.einsum(
            "erd,erf->edf", expert_in, grad_up_pre, preferred_element_type=jnp.float32
        )
        grad_in = jnp.einsum(
            "erf,edf->erd", grad_gate_pre, full_gate, preferred_element_type=jnp.float32
        ) + jnp.einsum("erf,edf->erd", grad_up_pre, full_up, preferred_element_type=jnp.float32)
        grad_normed_part = (
            jnp.zeros((row_count, model_width), jnp.float32)
            .at[source_rows]
            .add(grad_in.reshape(-1, model_width))
        )
        gate_grad_part = gate_slot_grad.reshape(-1)[slot_index].reshape(row_count, chosen_count)
        gate_grad = lax.psum(gate_grad_part, "tp")
        grad_probs = jnp.sum(picked * gate_grad[:, :, None], axis=1)
        grad_logits = (
            probs * (grad_probs - jnp.sum(probs * grad_probs, axis=-1, keepdims=True))
        ).astype(jnp.bfloat16)
        grad_router = jnp.einsum(
            "nd,ne->de", normed_ffn, grad_logits, preferred_element_type=jnp.float32
        )
        grad_normed = lax.psum(grad_normed_part, "tp") + jnp.einsum(
            "ne,de->nd", grad_logits, full_router, preferred_element_type=jnp.float32
        )
        grad_ffn_gain = jnp.sum(grad_normed * (middle * scale_two), axis=0)
        grad_middle = upstream + norm_back(grad_normed, middle, scale_two, ffn_vec)
        grad_branch = grad_middle.astype(jnp.bfloat16)
        grad_out_w = jnp.einsum(
            "nd,nc->dc", grad_branch, attended_low, preferred_element_type=jnp.float32
        )
        grad_att = jnp.einsum(
            "nd,dc->nc", grad_branch, full_out, preferred_element_type=jnp.float32
        ).reshape(shape_heads)
        grad_acc = (grad_att / per_row_total).astype(jnp.bfloat16)
        grad_total = jnp.transpose(-jnp.sum(grad_att * attended, axis=-1), (0, 2, 1)) / denominator
        grad_query, key_full, value_full = attend_backward(
            query, key_rows, value_send, grad_acc, grad_total
        )
        grad_keys, grad_values = (
            lax.psum_scatter(
                key_full.astype(jnp.bfloat16), "ctx", scatter_dimension=1, tiled=True
            ).astype(jnp.float32),
            lax.psum_scatter(
                value_full.astype(jnp.bfloat16), "ctx", scatter_dimension=1, tiled=True
            ).astype(jnp.float32),
        )
        grad_value_lin = grad_values.astype(jnp.bfloat16).reshape(row_count, -1)
        key_norm_grad = rotate(grad_keys.reshape(shape_heads), cosines, -sines)
        query_norm_grad = rotate(grad_query * score_scale, cosines, -sines)
        grad_qk_part = jnp.stack(
            [
                jnp.sum(query_norm_grad * query_hat, axis=(0, 1, 2)),
                jnp.sum(key_norm_grad * key_hat, axis=(0, 1, 2)),
            ],
            axis=1,
        )
        grad_query_lin = (
            norm_back(query_norm_grad, query_lin, query_scale, query_gain)
            .astype(jnp.bfloat16)
            .reshape(row_count, -1)
        )
        grad_key_lin = (
            norm_back(key_norm_grad, key_lin, key_scale, key_gain)
            .astype(jnp.bfloat16)
            .reshape(row_count, -1)
        )
        grad_query_w = jnp.einsum(
            "nd,nc->dc", normed, grad_query_lin, preferred_element_type=jnp.float32
        )
        grad_key_w = jnp.einsum(
            "nd,nc->dc", normed, grad_key_lin, preferred_element_type=jnp.float32
        )
        grad_value_w = jnp.einsum(
            "nd,nc->dc", normed, grad_value_lin, preferred_element_type=jnp.float32
        )
        grad_normed_attn = jnp.einsum(
            "nc,dc->nd", grad_query_lin, full_query, preferred_element_type=jnp.float32
        )
        grad_normed_attn = grad_normed_attn + jnp.einsum(
            "nc,dc->nd", grad_key_lin, full_key, preferred_element_type=jnp.float32
        )
        grad_normed_attn = grad_normed_attn + jnp.einsum(
            "nc,dc->nd", grad_value_lin, full_value, preferred_element_type=jnp.float32
        )
        grad_normed_one, grad_qk = (
            lax.psum(grad_normed_attn.astype(jnp.bfloat16), "tp").astype(jnp.float32),
            lax.psum(grad_qk_part.astype(jnp.bfloat16), "tp").astype(jnp.float32),
        )
        grad_attn_gain = jnp.sum(grad_normed_one * (inputs * scale_one), axis=0)
        grad_inputs = grad_middle + norm_back(grad_normed_one, inputs, scale_one, attn_vec)
        grad_parts.append(
            grad_inputs.astype(jnp.bfloat16).reshape(group_count, local_len, model_width)
        )
        dense_grads = (
            grad_attn_gain,
            grad_ffn_gain,
            grad_qk,
            grad_query_w,
            grad_key_w,
            grad_value_w,
            grad_out_w,
            grad_router,
        )
        expert_grads = (grad_gate_w, grad_up_w, grad_down_w)
        dense_total = add_all(dense_total, dense_grads)
        expert_total = add_all(expert_total, expert_grads)
    dense_owned, expert_owned = reduce_grads(dense_total, expert_total)
    layer_out = jnp.concatenate(out_parts, axis=0)
    input_grad = jnp.concatenate(grad_parts, axis=0)
    return (layer_out, input_grad) + tuple(dense_owned) + tuple(expert_owned)


def xor_permute(array, mask):
    return lax.ppermute(array, ("ctx", "tp"), [(i, i ^ mask) for i in range(32)])


BIT_K, BIT_Y, BIT_X, BIT_Z1, BIT_Z2 = 1, 2, 4, 8, 16


def with_partner(array, mask, axis):
    return jnp.concatenate([array, xor_permute(array, mask)], axis=axis)


def along_z(array, axis):
    return jnp.concatenate(
        [array] + [xor_permute(array, mask) for mask in (BIT_Z1, BIT_Z2, BIT_Z1 | BIT_Z2)], axis=axis
    )


def halve(array, mask, axis):
    half = array.shape[axis] // 2
    kept = lax.slice_in_dim(array, 0, half, axis=axis)
    sent = lax.slice_in_dim(array, half, 2 * half, axis=axis)
    return (kept.astype(jnp.float32) + xor_permute(sent, mask).astype(jnp.float32)).astype(jnp.bfloat16)


def sum_z(array, axis):
    size = array.shape[axis] // 4
    parts = [lax.slice_in_dim(array, i * size, (i + 1) * size, axis=axis) for i in range(4)]
    total = parts[0].astype(jnp.float32)
    for i, mask in ((1, BIT_Z1), (2, BIT_Z2), (3, BIT_Z1 | BIT_Z2)):
        total = total + xor_permute(parts[i], mask).astype(jnp.float32)
    return total


def gather_heads(owned):
    return with_partner(with_partner(along_z(owned, 1), BIT_Y, 1), BIT_K, 1)


def scatter_heads(partial):
    return sum_z(halve(halve(partial, BIT_K, 1), BIT_Y, 1), 1)


def gather_all(owned):
    first = along_z(owned[0], 0)
    second = along_z(owned[1], 0)
    first = with_partner(with_partner(first, BIT_X, 0), BIT_Y, 0)
    second = with_partner(with_partner(second, BIT_Y, 0), BIT_X, 0)
    return with_partner(first, BIT_K, 0), with_partner(second, BIT_K, 0)


def scatter_all(first, second):
    first = halve(first, BIT_K, 0)
    second = halve(second, BIT_K, 0)
    first = halve(halve(first, BIT_Y, 0), BIT_X, 0)
    second = halve(halve(second, BIT_X, 0), BIT_Y, 0)
    return jnp.stack([sum_z(first, 0), sum_z(second, 0)], 0)


def exchange(array):
    return lax.all_to_all(array, "ctx", 0, 0, tiled=True)


def per_device_fast(
    tokens, cotangent, routes, attn_gain, ffn_gain, qk_gain, w_query, w_key, w_value, w_out, router, w_gate, w_up, w_down
):
    width = tokens.shape[2]
    head_size = qk_gain.shape[0] * 8
    half_size = head_size // 2
    experts = w_gate.shape[0]
    mine = experts // 8
    hidden_units = w_gate.shape[2]
    ctx, tp = lax.axis_index("ctx"), lax.axis_index("tp")
    z, x, y, k = ctx // 2, ctx % 2, tp // 2, tp % 2
    f32, bf16 = jnp.float32, jnp.bfloat16

    pack = jnp.zeros((256, 20), bf16)
    pack = pack.at[:, :experts].set(router).at[:, 16].set(attn_gain).at[:, 17].set(ffn_gain)
    pack = pack.at[:16, 18:20].set(qk_gain)
    pack = lax.all_gather(pack, "ctx", axis=0, tiled=True)
    full_router = pack[:, :16]
    attn_vec, ffn_vec = pack[:, 16].astype(f32), pack[:, 17].astype(f32)
    qk_full = pack.reshape(8, 256, 20)[:, :16, 18:20].reshape(head_size, 2).astype(f32)
    query_gain, key_gain = qk_full[:, 0], qk_full[:, 1]
    all_routes = lax.all_gather(routes, "ctx", axis=1, tiled=True)

    def own_rows(array):
        rows = lax.dynamic_slice_in_dim(array, tp * 16, 16, 1)
        kept = lax.dynamic_slice_in_dim(rows, 2 * x, 2, 0)
        sent = lax.dynamic_slice_in_dim(rows, 2 - 2 * x, 2, 0)
        return jnp.concatenate([kept, xor_permute(sent, BIT_X)], axis=1)

    own_tokens = own_rows(tokens)
    own_cot = own_rows(cotangent)
    head_tokens = gather_heads(own_tokens)

    dense = jnp.stack([w_query, w_key, w_value, w_out], 0).reshape(4, 256, 4, head_size)
    dense = jnp.transpose(dense, (2, 1, 0, 3))
    dense = jnp.repeat(dense, 2, axis=0)
    dense = exchange(dense).reshape(width, 4, head_size)
    w_qkv = dense[:, :3].reshape(width, 3 * head_size)
    w_o = dense[:, 3]

    def fetch(weight):
        weight = exchange(weight.reshape(8, mine, 256, hidden_units))
        return jnp.transpose(weight, (0, 2, 1, 3)).reshape(width, mine * hidden_units)

    gate_w, up_w, down_w = fetch(w_gate), fetch(w_up), fetch(w_down)

    cot_first, cot_second = gather_all(own_cot)
    dm = jnp.concatenate([cot_first, cot_second], 0)

    def bits(*shape):
        return [lax.broadcasted_iota(jnp.int32, shape, i) for i in range(len(shape))]

    dk, dy, dz, dx, i = bits(2, 2, 4, 2, 16)
    positions = ((z ^ dz) * 2 + (x ^ dx)) * 64 + ((y ^ dy) * 2 + (k ^ dk)) * 16 + i
    positions = positions.reshape(512).astype(f32)
    frequencies = ROPE_BASE ** (-2.0 * jnp.arange(half_size).astype(f32) / head_size)
    angles = positions[:, None] * frequencies[None, :]
    cosines, sines = jnp.cos(angles)[None], jnp.sin(angles)[None]

    def token_of(part, dx_dev, dy, dz, dk, dx_block, i):
        return (2 * (x ^ dx_dev) + part) * 512 + ((z ^ dz) * 2 + (x ^ dx_dev ^ dx_block)) * 64 + ((y ^ dy) * 2 + (k ^ dk)) * 16 + i

    dk, dy, dx, dz, db, i = bits(2, 2, 2, 4, 2, 16)
    rows_first = token_of(0, dx, dy, dz, dk, db, i).reshape(-1)
    dk, dx, dy, dz, db, i = bits(2, 2, 2, 4, 2, 16)
    rows_second = token_of(1, dx, dy, dz, dk, db, i).reshape(-1)
    row_tokens = jnp.concatenate([rows_first, rows_second], 0)
    row_routes = jnp.take(all_routes.reshape(-1, routes.shape[2]), row_tokens, axis=0)
    chosen = jnp.sum((row_routes[:, :, None] == jnp.arange(experts)[None, None, :]).astype(f32), axis=1)

    inputs = head_tokens.astype(f32)
    scale_one = inverse_rms(inputs)
    unit = inputs * scale_one
    normed = (unit * attn_vec).astype(bf16)
    lin = product(normed, w_qkv)
    query_lin, key_lin = lin[..., :head_size], lin[..., head_size : 2 * head_size]
    value_rows = lin[..., 2 * head_size :].astype(bf16)
    score_scale = head_size ** (-0.5)
    query_scale, key_scale = inverse_rms(query_lin), inverse_rms(key_lin)
    query_hat, key_hat = query_lin * query_scale, key_lin * key_scale
    query = (rotate(query_hat * query_gain, cosines, sines) * score_scale).astype(bf16)
    keys = rotate(key_hat * key_gain, cosines, sines).astype(bf16)
    scores = jnp.einsum("sqd,skd->sqk", query, keys, preferred_element_type=f32)
    exponent = jnp.exp(scores)
    denominator = jnp.sum(exponent, axis=-1, keepdims=True)
    expo_low = exponent.astype(bf16)
    attended = jnp.einsum("sqk,skd->sqd", expo_low, value_rows, preferred_element_type=f32) / denominator
    attended_low = attended.astype(bf16)
    branch_part = jnp.einsum("snc,dc->snd", attended_low, w_o, preferred_element_type=f32).astype(bf16)
    middle = own_tokens.astype(f32) + scatter_heads(branch_part)

    scale_two = inverse_rms(middle)
    unit_two = middle * scale_two
    normed_ffn = (unit_two * ffn_vec).astype(bf16)
    nf = jnp.concatenate(gather_all(normed_ffn), 0)
    probs = jax.nn.softmax(product(nf, full_router), axis=-1)
    own_probs = lax.dynamic_slice_in_dim(probs, mine * ctx, mine, 1)
    own_chosen = lax.dynamic_slice_in_dim(chosen, mine * ctx, mine, 1)
    gates = own_probs * own_chosen
    rows = nf.shape[0]

    def spread(columns):
        return jnp.broadcast_to(columns[:, :, None], (rows, mine, hidden_units)).reshape(rows, mine * hidden_units)

    gate_pre, up_pre = product(nf, gate_w), product(nf, up_w)
    sigmoid_gate = jax.nn.sigmoid(gate_pre)
    silu_gate = gate_pre * sigmoid_gate
    activated = silu_gate * up_pre
    gate_wide = spread(gates)
    hidden = (gate_wide * activated).astype(bf16)
    mixed_part = jnp.einsum("nf,df->nd", hidden, down_w, preferred_element_type=f32).astype(bf16)
    half_rows = rows // 2
    mixed = scatter_all(mixed_part[:half_rows], mixed_part[half_rows:])
    layer_out = (middle + mixed).astype(bf16)

    grad_hidden = product(dm, down_w)
    gate_grad = jnp.sum((grad_hidden * activated).reshape(rows, mine, hidden_units), axis=-1) * own_chosen
    grad_act = gate_wide * grad_hidden
    grad_up_pre = (grad_act * silu_gate).astype(bf16)
    grad_gate_pre = (grad_act * up_pre * sigmoid_gate * (1.0 + gate_pre * (1.0 - sigmoid_gate))).astype(bf16)
    own_ids = mine * ctx + jnp.arange(mine)
    placed = jnp.sum(gate_grad[:, :, None] * (own_ids[:, None] == jnp.arange(experts)[None, :]).astype(f32), axis=1)
    grad_logits = (probs * (placed - jnp.sum(probs * placed, axis=-1, keepdims=True))).astype(bf16)
    grad_normed_part = (
        jnp.einsum("nf,df->nd", grad_gate_pre, gate_w, preferred_element_type=f32)
        + jnp.einsum("nf,df->nd", grad_up_pre, up_w, preferred_element_type=f32)
        + jnp.einsum("ne,de->nd", grad_logits, full_router, preferred_element_type=f32)
    ).astype(bf16)
    grad_normed = scatter_all(grad_normed_part[:half_rows], grad_normed_part[half_rows:])

    def transposed(left_op, right_op):
        return jnp.einsum("nd,nf->df", left_op, right_op, preferred_element_type=f32)

    def give_back(gradient):
        gradient = gradient.astype(bf16).reshape(8, 256, mine, hidden_units)
        gradient = exchange(jnp.transpose(gradient, (0, 2, 1, 3)))
        return gradient.reshape(experts, 256, hidden_units).astype(f32)

    grad_down_w = give_back(transposed(dm, hidden))
    grad_gate_w = give_back(transposed(nf, grad_gate_pre))
    grad_up_w = give_back(transposed(nf, grad_up_pre))
    grad_router_part = transposed(nf, grad_logits)

    upstream = own_cot.astype(f32)
    grad_ffn_part = jnp.sum(grad_normed * unit_two, axis=(0, 1))
    grad_middle = upstream + norm_back(grad_normed, middle, scale_two, ffn_vec)

    grad_branch = gather_heads(grad_middle.astype(bf16))
    grad_att = product(grad_branch, w_o)
    grad_out_part = jnp.einsum("snd,snc->dc", grad_branch, attended_low, preferred_element_type=f32)
    grad_acc = (grad_att / denominator).astype(bf16)
    grad_total = -jnp.sum(grad_att * attended, axis=-1, keepdims=True) / denominator
    grad_prob = jnp.einsum("sqd,skd->sqk", grad_acc, value_rows, preferred_element_type=f32)
    grad_score = (exponent * (grad_prob + grad_total)).astype(bf16)
    grad_query = jnp.einsum("sqk,skd->sqd", grad_score, keys, preferred_element_type=f32)
    grad_keys = jnp.einsum("sqk,sqd->skd", grad_score, query, preferred_element_type=f32)
    grad_values = jnp.einsum("sqk,sqd->skd", expo_low, grad_acc, preferred_element_type=f32)
    query_norm_grad = rotate(grad_query * score_scale, cosines, -sines)
    key_norm_grad = rotate(grad_keys, cosines, -sines)
    grad_qk_part = jnp.stack(
        [jnp.sum(query_norm_grad * query_hat, axis=(0, 1)), jnp.sum(key_norm_grad * key_hat, axis=(0, 1))], axis=1
    )
    grad_lin = jnp.concatenate(
        [
            norm_back(query_norm_grad, query_lin, query_scale, query_gain).astype(bf16),
            norm_back(key_norm_grad, key_lin, key_scale, key_gain).astype(bf16),
            grad_values.astype(bf16),
        ],
        axis=-1,
    )
    grad_normed_attn = jnp.einsum("snc,dc->snd", grad_lin, w_qkv, preferred_element_type=f32)
    grad_attn_part = jnp.sum(grad_normed_attn * unit, axis=(0, 1))
    grad_normed_one = scatter_heads(grad_normed_attn.astype(bf16))
    own_inputs = own_tokens.astype(f32)
    grad_inputs = grad_middle + norm_back(grad_normed_one, own_inputs, inverse_rms(own_inputs), attn_vec)

    grad_qkv_part = jnp.einsum("snd,snc->dc", normed, grad_lin, preferred_element_type=f32)
    dense_grad = jnp.concatenate([grad_qkv_part, grad_out_part], axis=1).astype(bf16).reshape(8, 256, 4, head_size)
    dense_grad = exchange(dense_grad).astype(f32).reshape(4, 2, 256, 4, head_size).sum(1)
    dense_grad = jnp.transpose(dense_grad, (2, 1, 0, 3)).reshape(4, 256, 4 * head_size)

    small = jnp.zeros((width, 20), f32)
    small = small.at[:, :16].set(grad_router_part).at[:, 16].set(grad_attn_part).at[:, 17].set(grad_ffn_part)
    small = small.reshape(8, 256, 20).at[:, :16, 18:20].set(grad_qk_part.reshape(8, 16, 2)).reshape(width, 20)
    small = lax.psum(lax.psum_scatter(small, "ctx", scatter_dimension=0, tiled=True), "tp")

    def hand_out(owned):
        kept, received = owned[:, :16], xor_permute(owned[:, 16:], BIT_X)
        rows = jnp.where(x == 0, jnp.concatenate([kept, received], 0), jnp.concatenate([received, kept], 0))
        return lax.all_gather(rows, "tp", axis=1, tiled=True)

    return (
        hand_out(layer_out),
        hand_out(grad_inputs.astype(bf16)),
        small[:, 16],
        small[:, 17],
        small[:16, 18:20],
        dense_grad[0],
        dense_grad[1],
        dense_grad[2],
        dense_grad[3],
        small[:, :16],
        grad_gate_w,
        grad_up_w,
        grad_down_w,
    )


def solution(mesh):
    fast = mesh.shape["ctx"] == 8 and mesh.shape["tp"] == 4
    return jax.shard_map(
        per_device_fast if fast else per_device,
        mesh=mesh,
        in_specs=(
            P(None, "ctx", None),
            P(None, "ctx", None),
            P(None, "ctx", None),
            P("ctx"),
            P("ctx"),
            P("ctx", None),
            P("ctx", "tp"),
            P("ctx", "tp"),
            P("ctx", "tp"),
            P("ctx", "tp"),
            P("ctx", None),
            P(None, "ctx", "tp"),
            P(None, "ctx", "tp"),
            P(None, "ctx", "tp"),
        ),
        out_specs=(
            P(None, "ctx", None),
            P(None, "ctx", None),
            P("ctx"),
            P("ctx"),
            P("ctx", None),
            P("ctx", "tp"),
            P("ctx", "tp"),
            P("ctx", "tp"),
            P("ctx", "tp"),
            P("ctx", None),
            P(None, "ctx", "tp"),
            P(None, "ctx", "tp"),
            P(None, "ctx", "tp"),
        ),
        check_vma=False,
    )
```

```python
import jax
import jax.numpy as jnp
import numpy as np
from jax import lax
from jax.experimental import pallas as pl
from jax.experimental.pallas import tpu as pltpu
from jax.sharding import PartitionSpec as P

MICRO = 2
MOST = 48


EPS = 1e-06
ROPE_BASE = 50000.0


def product(left_op, right_op):
    return jnp.dot(left_op, right_op, preferred_element_type=jnp.float32)


def rotate(values, cosines, sines):
    half_size = values.shape[-1] // 2
    first_half = values[..., :half_size]
    second_half = values[..., half_size:]
    return jnp.concatenate(
        [first_half * cosines - second_half * sines, second_half * cosines + first_half * sines],
        axis=-1,
    )


def inverse_rms(values):
    return lax.rsqrt(jnp.mean(values * values, axis=-1, keepdims=True) + EPS)


def norm_back(gradient, inputs, scaling, gain_vec):
    weighted = gradient * gain_vec
    return scaling * weighted - inputs * scaling**3 * jnp.mean(
        weighted * inputs, axis=-1, keepdims=True
    )


def fetch_dense(attn_gain, ffn_gain, qk_gain, w_query, w_key, w_value, w_out, router):
    return (
        lax.all_gather(attn_gain, "ctx", axis=0, tiled=True),
        lax.all_gather(ffn_gain, "ctx", axis=0, tiled=True),
        lax.all_gather(qk_gain, "ctx", axis=0, tiled=True),
        lax.all_gather(w_query, "ctx", axis=0, tiled=True),
        lax.all_gather(w_key, "ctx", axis=0, tiled=True),
        lax.all_gather(w_value, "ctx", axis=0, tiled=True),
        lax.all_gather(w_out, "ctx", axis=0, tiled=True),
        lax.all_gather(router, "ctx", axis=0, tiled=True),
    )


def fetch_experts(w_gate, w_up, w_down):
    return (
        lax.all_gather(w_gate, "ctx", axis=1, tiled=True),
        lax.all_gather(w_up, "ctx", axis=1, tiled=True),
        lax.all_gather(w_down, "ctx", axis=1, tiled=True),
    )


def reduce_grads(dense_grads, expert_grads):
    dense_owned = (
        lax.psum_scatter(
            dense_grads[0].astype(jnp.bfloat16), "ctx", scatter_dimension=0, tiled=True
        ).astype(jnp.float32),
        lax.psum_scatter(
            dense_grads[1].astype(jnp.bfloat16), "ctx", scatter_dimension=0, tiled=True
        ).astype(jnp.float32),
        lax.psum_scatter(
            dense_grads[2].astype(jnp.bfloat16), "ctx", scatter_dimension=0, tiled=True
        ).astype(jnp.float32),
        lax.psum_scatter(
            dense_grads[3].astype(jnp.bfloat16), "ctx", scatter_dimension=0, tiled=True
        ).astype(jnp.float32),
        lax.psum_scatter(
            dense_grads[4].astype(jnp.bfloat16), "ctx", scatter_dimension=0, tiled=True
        ).astype(jnp.float32),
        lax.psum_scatter(
            dense_grads[5].astype(jnp.bfloat16), "ctx", scatter_dimension=0, tiled=True
        ).astype(jnp.float32),
        lax.psum_scatter(
            dense_grads[6].astype(jnp.bfloat16), "ctx", scatter_dimension=0, tiled=True
        ).astype(jnp.float32),
        lax.psum_scatter(
            dense_grads[7].astype(jnp.bfloat16), "ctx", scatter_dimension=0, tiled=True
        ).astype(jnp.float32),
    )
    expert_owned = (
        lax.psum_scatter(
            expert_grads[0].astype(jnp.bfloat16), "ctx", scatter_dimension=1, tiled=True
        ).astype(jnp.float32),
        lax.psum_scatter(
            expert_grads[1].astype(jnp.bfloat16), "ctx", scatter_dimension=1, tiled=True
        ).astype(jnp.float32),
        lax.psum_scatter(
            expert_grads[2].astype(jnp.bfloat16), "ctx", scatter_dimension=1, tiled=True
        ).astype(jnp.float32),
    )
    return (tuple(dense_owned), tuple(expert_owned))


def add_all(earlier, latest):
    if earlier is None:
        return latest
    return tuple((first_one + second_one for first_one, second_one in zip(earlier, latest)))


def attend_forward(query, key_rows, value_rows):
    batch_count, query_count, head_count, head_size = query.shape

    def add_piece(state_pair, pieces, offset):
        key_piece = pieces[0].reshape(batch_count, -1, head_count, head_size)
        value_piece = pieces[1].reshape(batch_count, -1, head_count, head_size)
        scores = jnp.einsum("bqhd,bkhd->bhqk", query, key_piece, preferred_element_type=jnp.float32)
        exponent = jnp.exp(scores)
        denominator = jnp.sum(exponent, axis=-1)
        accum_sum = jnp.einsum(
            "bhqk,bkhd->bqhd",
            exponent.astype(jnp.bfloat16),
            value_piece,
            preferred_element_type=jnp.float32,
        )
        return (accum_sum, denominator)

    initial = (
        jnp.zeros(query.shape, jnp.float32),
        jnp.zeros((batch_count, head_count, query_count), jnp.float32),
    )
    return add_piece(
        initial,
        (
            lax.all_gather(key_rows, "ctx", axis=1, tiled=True),
            lax.all_gather(value_rows, "ctx", axis=1, tiled=True),
        ),
        jnp.int32(0),
    )


def attend_backward(query, key_rows, value_rows, grad_acc, grad_total):
    batch_count, query_count, head_count, head_size = query.shape
    full_len = key_rows.shape[1] * lax.axis_size("ctx")

    def add_piece(state_three, pieces, offset):
        key_piece = pieces[0].reshape(batch_count, -1, head_count, head_size)
        value_piece = pieces[1].reshape(batch_count, -1, head_count, head_size)
        piece_len = key_piece.shape[1]
        scores = jnp.einsum("bqhd,bkhd->bhqk", query, key_piece, preferred_element_type=jnp.float32)
        exponent = jnp.exp(scores)
        grad_prob = jnp.einsum(
            "bqhd,bkhd->bhqk", grad_acc, value_piece, preferred_element_type=jnp.float32
        )
        grad_score = (exponent * (grad_prob + grad_total[..., None])).astype(jnp.bfloat16)
        grad_query = jnp.einsum(
            "bhqk,bkhd->bqhd", grad_score, key_piece, preferred_element_type=jnp.float32
        )
        key_term = jnp.einsum(
            "bhqk,bqhd->bkhd", grad_score, query, preferred_element_type=jnp.float32
        ).reshape(batch_count, piece_len, -1)
        value_term = jnp.einsum(
            "bhqk,bqhd->bkhd",
            exponent.astype(jnp.bfloat16),
            grad_acc,
            preferred_element_type=jnp.float32,
        ).reshape(batch_count, piece_len, -1)
        return (grad_query, key_term, value_term)

    initial = (jnp.zeros(query.shape, jnp.float32),)
    initial = initial + (
        jnp.zeros((batch_count, full_len, head_count * head_size), jnp.float32),
        jnp.zeros((batch_count, full_len, head_count * head_size), jnp.float32),
    )
    return add_piece(
        initial,
        (
            lax.all_gather(key_rows, "ctx", axis=1, tiled=True),
            lax.all_gather(value_rows, "ctx", axis=1, tiled=True),
        ),
        jnp.int32(0),
    )


def dispatch(route_block, gate_item, expert_count):
    group_count, local_len, chosen_count = route_block.shape
    expert_ids = route_block.reshape(group_count, local_len * chosen_count)
    onehot = (expert_ids[..., None] == jnp.arange(expert_count)[None, None, :]).astype(jnp.int32)
    before = jnp.cumsum(onehot, axis=1) - onehot
    position = jnp.sum(before * onehot, axis=2)
    slot_index = (
        expert_ids * (group_count * MOST) + jnp.arange(group_count)[:, None] * MOST + position
    )
    owner_row = (
        jnp.arange(group_count)[:, None] * local_len
        + jnp.arange(local_len * chosen_count)[None, :] // chosen_count
    )
    slot_index = slot_index.reshape(-1)
    source_rows = (
        jnp.zeros(expert_count * group_count * MOST, jnp.int32)
        .at[slot_index]
        .set(owner_row.reshape(-1))
    )
    gate_slot = (
        jnp.zeros(expert_count * group_count * MOST, jnp.float32)
        .at[slot_index]
        .set(gate_item.reshape(-1))
    )
    return (slot_index, source_rows, gate_slot)


def per_device(
    tokens,
    cotangent,
    routes,
    attn_gain,
    ffn_gain,
    qk_gain,
    w_query,
    w_key,
    w_value,
    w_out,
    router,
    w_gate,
    w_up,
    w_down,
):
    sequences, local_len, model_width = tokens.shape
    head_size = qk_gain.shape[0] * lax.axis_size("ctx")
    head_count = w_query.shape[1] // head_size
    expert_count = w_gate.shape[0]
    chosen_count = routes.shape[2]
    group_count = sequences // MICRO
    row_count = group_count * local_len
    half_size = head_size // 2
    positions = (lax.axis_index("ctx") * local_len + jnp.arange(local_len)).astype(jnp.float32)
    frequencies = ROPE_BASE ** (-2.0 * jnp.arange(half_size).astype(jnp.float32) / head_size)
    angles = positions[:, None] * frequencies[None, :]
    cosines = jnp.cos(angles)[None, :, None, :]
    sines = jnp.sin(angles)[None, :, None, :]
    score_scale = head_size ** (-0.5)
    shape_heads = (group_count, local_len, head_count, head_size)
    dense_total = None
    expert_total = None
    out_parts = []
    grad_parts = []
    for micro_step in range(MICRO):
        first_seq = micro_step * group_count
        inputs = (
            tokens[first_seq : first_seq + group_count]
            .astype(jnp.float32)
            .reshape(row_count, model_width)
        )
        route_block = routes[first_seq : first_seq + group_count]
        upstream = (
            cotangent[first_seq : first_seq + group_count]
            .astype(jnp.float32)
            .reshape(row_count, model_width)
        )
        gain_attn, gain_ffn, gain_qk, full_query, full_key, full_value, full_out, full_router = (
            fetch_dense(attn_gain, ffn_gain, qk_gain, w_query, w_key, w_value, w_out, router)
        )
        full_gate, full_up, full_down = fetch_experts(w_gate, w_up, w_down)
        attn_vec = gain_attn.astype(jnp.float32)
        ffn_vec = gain_ffn.astype(jnp.float32)
        query_gain = gain_qk[:, 0].astype(jnp.float32)
        key_gain = gain_qk[:, 1].astype(jnp.float32)
        scale_one = inverse_rms(inputs)
        normed = (inputs * scale_one * attn_vec).astype(jnp.bfloat16)
        query_lin = product(normed, full_query).reshape(shape_heads)
        key_lin = product(normed, full_key).reshape(shape_heads)
        value_send = (
            product(normed, full_value).astype(jnp.bfloat16).reshape(group_count, local_len, -1)
        )
        query_scale = inverse_rms(query_lin)
        key_scale = inverse_rms(key_lin)
        query_hat = query_lin * query_scale
        key_hat = key_lin * key_scale
        query = (rotate(query_hat * query_gain, cosines, sines) * score_scale).astype(jnp.bfloat16)
        key_rows = (
            rotate(key_hat * key_gain, cosines, sines)
            .astype(jnp.bfloat16)
            .reshape(group_count, local_len, -1)
        )
        accum_sum, denominator = attend_forward(query, key_rows, value_send)
        per_row_total = jnp.transpose(denominator, (0, 2, 1))[..., None]
        attended = accum_sum / per_row_total
        attended_low = attended.astype(jnp.bfloat16).reshape(row_count, -1)
        branch = lax.psum(
            jnp.einsum("nc,dc->nd", attended_low, full_out, preferred_element_type=jnp.float32),
            "tp",
        )
        middle = inputs + branch
        scale_two = inverse_rms(middle)
        normed_ffn = (middle * scale_two * ffn_vec).astype(jnp.bfloat16)
        logits = product(normed_ffn, full_router)
        probs = jax.nn.softmax(logits, axis=-1)
        route_flat = route_block.reshape(row_count, chosen_count)
        picked = (route_flat[:, :, None] == jnp.arange(expert_count)[None, None, :]).astype(
            jnp.float32
        )
        gate_item = jnp.sum(picked * probs[:, None, :], axis=-1)
        slot_index, source_rows, gate_slot = dispatch(route_block, gate_item, expert_count)
        expert_in = normed_ffn[source_rows].reshape(expert_count, -1, model_width)
        gate_pre = jnp.einsum(
            "erd,edf->erf", expert_in, full_gate, preferred_element_type=jnp.float32
        )
        up_pre = jnp.einsum("erd,edf->erf", expert_in, full_up, preferred_element_type=jnp.float32)
        activated = jax.nn.silu(gate_pre) * up_pre
        gate_col = gate_slot.reshape(expert_count, -1)[:, :, None]
        hidden = (gate_col * activated).astype(jnp.bfloat16)
        expert_out = jnp.einsum(
            "erf,edf->erd", hidden, full_down, preferred_element_type=jnp.float32
        )
        mixed_part = (
            jnp.zeros((row_count, model_width), jnp.float32)
            .at[source_rows]
            .add(expert_out.reshape(-1, model_width))
        )
        mixed = lax.psum(mixed_part.astype(jnp.bfloat16), "tp").astype(jnp.float32)
        out_parts.append(
            (middle + mixed).astype(jnp.bfloat16).reshape(group_count, local_len, model_width)
        )
        gain_attn, gain_ffn, gain_qk, full_query, full_key, full_value, full_out, full_router = (
            fetch_dense(attn_gain, ffn_gain, qk_gain, w_query, w_key, w_value, w_out, router)
        )
        full_gate, full_up, full_down = fetch_experts(w_gate, w_up, w_down)
        grad_mixed = upstream.astype(jnp.bfloat16)
        grad_rows = grad_mixed[source_rows].reshape(expert_count, -1, model_width)
        grad_down_w = jnp.einsum(
            "erd,erf->edf", grad_rows, hidden, preferred_element_type=jnp.float32
        )
        grad_hidden = jnp.einsum(
            "erd,edf->erf", grad_rows, full_down, preferred_element_type=jnp.float32
        )
        gate_slot_grad = jnp.sum(grad_hidden * activated, axis=-1)
        grad_act = gate_col * grad_hidden
        sigmoid_gate = jax.nn.sigmoid(gate_pre)
        grad_up_pre = (grad_act * jax.nn.silu(gate_pre)).astype(jnp.bfloat16)
        grad_gate_pre = (
            grad_act * up_pre * sigmoid_gate * (1.0 + gate_pre * (1.0 - sigmoid_gate))
        ).astype(jnp.bfloat16)
        grad_gate_w = jnp.einsum(
            "erd,erf->edf", expert_in, grad_gate_pre, preferred_element_type=jnp.float32
        )
        grad_up_w = jnp.einsum(
            "erd,erf->edf", expert_in, grad_up_pre, preferred_element_type=jnp.float32
        )
        grad_in = jnp.einsum(
            "erf,edf->erd", grad_gate_pre, full_gate, preferred_element_type=jnp.float32
        ) + jnp.einsum("erf,edf->erd", grad_up_pre, full_up, preferred_element_type=jnp.float32)
        grad_normed_part = (
            jnp.zeros((row_count, model_width), jnp.float32)
            .at[source_rows]
            .add(grad_in.reshape(-1, model_width))
        )
        gate_grad_part = gate_slot_grad.reshape(-1)[slot_index].reshape(row_count, chosen_count)
        gate_grad = lax.psum(gate_grad_part, "tp")
        grad_probs = jnp.sum(picked * gate_grad[:, :, None], axis=1)
        grad_logits = (
            probs * (grad_probs - jnp.sum(probs * grad_probs, axis=-1, keepdims=True))
        ).astype(jnp.bfloat16)
        grad_router = jnp.einsum(
            "nd,ne->de", normed_ffn, grad_logits, preferred_element_type=jnp.float32
        )
        grad_normed = lax.psum(grad_normed_part, "tp") + jnp.einsum(
            "ne,de->nd", grad_logits, full_router, preferred_element_type=jnp.float32
        )
        grad_ffn_gain = jnp.sum(grad_normed * (middle * scale_two), axis=0)
        grad_middle = upstream + norm_back(grad_normed, middle, scale_two, ffn_vec)
        grad_branch = grad_middle.astype(jnp.bfloat16)
        grad_out_w = jnp.einsum(
            "nd,nc->dc", grad_branch, attended_low, preferred_element_type=jnp.float32
        )
        grad_att = jnp.einsum(
            "nd,dc->nc", grad_branch, full_out, preferred_element_type=jnp.float32
        ).reshape(shape_heads)
        grad_acc = (grad_att / per_row_total).astype(jnp.bfloat16)
        grad_total = jnp.transpose(-jnp.sum(grad_att * attended, axis=-1), (0, 2, 1)) / denominator
        grad_query, key_full, value_full = attend_backward(
            query, key_rows, value_send, grad_acc, grad_total
        )
        grad_keys, grad_values = (
            lax.psum_scatter(
                key_full.astype(jnp.bfloat16), "ctx", scatter_dimension=1, tiled=True
            ).astype(jnp.float32),
            lax.psum_scatter(
                value_full.astype(jnp.bfloat16), "ctx", scatter_dimension=1, tiled=True
            ).astype(jnp.float32),
        )
        grad_value_lin = grad_values.astype(jnp.bfloat16).reshape(row_count, -1)
        key_norm_grad = rotate(grad_keys.reshape(shape_heads), cosines, -sines)
        query_norm_grad = rotate(grad_query * score_scale, cosines, -sines)
        grad_qk_part = jnp.stack(
            [
                jnp.sum(query_norm_grad * query_hat, axis=(0, 1, 2)),
                jnp.sum(key_norm_grad * key_hat, axis=(0, 1, 2)),
            ],
            axis=1,
        )
        grad_query_lin = (
            norm_back(query_norm_grad, query_lin, query_scale, query_gain)
            .astype(jnp.bfloat16)
            .reshape(row_count, -1)
        )
        grad_key_lin = (
            norm_back(key_norm_grad, key_lin, key_scale, key_gain)
            .astype(jnp.bfloat16)
            .reshape(row_count, -1)
        )
        grad_query_w = jnp.einsum(
            "nd,nc->dc", normed, grad_query_lin, preferred_element_type=jnp.float32
        )
        grad_key_w = jnp.einsum(
            "nd,nc->dc", normed, grad_key_lin, preferred_element_type=jnp.float32
        )
        grad_value_w = jnp.einsum(
            "nd,nc->dc", normed, grad_value_lin, preferred_element_type=jnp.float32
        )
        grad_normed_attn = jnp.einsum(
            "nc,dc->nd", grad_query_lin, full_query, preferred_element_type=jnp.float32
        )
        grad_normed_attn = grad_normed_attn + jnp.einsum(
            "nc,dc->nd", grad_key_lin, full_key, preferred_element_type=jnp.float32
        )
        grad_normed_attn = grad_normed_attn + jnp.einsum(
            "nc,dc->nd", grad_value_lin, full_value, preferred_element_type=jnp.float32
        )
        grad_normed_one, grad_qk = (
            lax.psum(grad_normed_attn.astype(jnp.bfloat16), "tp").astype(jnp.float32),
            lax.psum(grad_qk_part.astype(jnp.bfloat16), "tp").astype(jnp.float32),
        )
        grad_attn_gain = jnp.sum(grad_normed_one * (inputs * scale_one), axis=0)
        grad_inputs = grad_middle + norm_back(grad_normed_one, inputs, scale_one, attn_vec)
        grad_parts.append(
            grad_inputs.astype(jnp.bfloat16).reshape(group_count, local_len, model_width)
        )
        dense_grads = (
            grad_attn_gain,
            grad_ffn_gain,
            grad_qk,
            grad_query_w,
            grad_key_w,
            grad_value_w,
            grad_out_w,
            grad_router,
        )
        expert_grads = (grad_gate_w, grad_up_w, grad_down_w)
        dense_total = add_all(dense_total, dense_grads)
        expert_total = add_all(expert_total, expert_grads)
    dense_owned, expert_owned = reduce_grads(dense_total, expert_total)
    layer_out = jnp.concatenate(out_parts, axis=0)
    input_grad = jnp.concatenate(grad_parts, axis=0)
    return (layer_out, input_grad) + tuple(dense_owned) + tuple(expert_owned)


MESH_ID = pl.DeviceIdType.MESH
F32, BF16 = jnp.float32, jnp.bfloat16
VMEM_LIMIT = 63 * 1024 * 1024


class Place:
    def __init__(self, z, x, y, k):
        self.z, self.x, self.y, self.k = z, x, y, k
        self.ctx, self.tp = z * 2 + x, y * 2 + k
        self.owner32 = self.ctx * 4 + self.tp
        self.owner16 = z * 4 + self.tp
        self.owner8 = x * 4 + self.tp
        self.device = (self.ctx, self.tp)

    def flip(self, dims):
        z, x, y, k = self.z, self.x, self.y, self.k
        for dim in dims:
            if dim == "Z":
                z = z + 2 - 4 * (z // 2)
            elif dim == "z":
                z = z + 1 - 2 * (z % 2)
            elif dim == "x":
                x = 1 - x
            elif dim == "y":
                y = 1 - y
            else:
                k = 1 - k
        return Place(z, x, y, k)


def my_place():
    ctx, tp = lax.axis_index("ctx"), lax.axis_index("tp")
    return Place(ctx // 2, ctx % 2, tp // 2, tp % 2)


def ctx_peer(here, step):
    ctx = (here.ctx + step) % 8
    return Place(ctx // 2, ctx % 2, here.y, here.k)


def everyone(here):
    return [ctx_peer(here, step) for step in range(1, 8)] + [here.flip("y"), here.flip("k")]


def greet(here):
    barrier = pltpu.get_barrier_semaphore()
    peers = everyone(here)
    for peer in peers:
        pl.semaphore_signal(barrier, inc=1, device_id=peer.device, device_id_type=MESH_ID)
    pl.semaphore_wait(barrier, len(peers))


def remote(source, target, send_sem, recv_sem, peer):
    return pltpu.make_async_remote_copy(
        src_ref=source,
        dst_ref=target,
        send_sem=send_sem,
        recv_sem=recv_sem,
        device_id=peer.device,
        device_id_type=MESH_ID,
    )


def subsets(dims):
    found = [""]
    for dim in dims:
        found = found + [one + dim for one in found]
    return sorted(found, key=len)


class Gather:
    def __init__(self, here, dims, slot, send_sems, recv_sems, own=None):
        self.here, self.dims, self.slot, self.own = here, dims, slot, own
        self.send_sems, self.recv_sems = send_sems, recv_sems
        self.started = []

    def number(self, r):
        return sum(1 << self.dims.index(dim) for dim in r)

    def copy(self, r, dim):
        block = self.slot(self.here.flip(r))
        source = self.own if (r == "" and self.own is not None) else block
        i = self.number(r + dim)
        return remote(source, block, self.send_sems.at[i], self.recv_sems.at[i], self.here.flip(dim))

    def send(self, r):
        last = max([self.dims.index(dim) for dim in r], default=-1)
        for dim in self.dims[last + 1 :]:
            copy = self.copy(r, dim)
            copy.start()
            self.started.append(copy)

    def arrive(self, r):
        block = self.slot(self.here.flip(r))
        i = self.number(r)
        last = self.dims[max(self.dims.index(dim) for dim in r)]
        remote(block, block, self.send_sems.at[i], self.recv_sems.at[i], self.here.flip(last)).wait_recv()
        self.send(r)

    def sort(self, r):
        return "".join(dim for dim in self.dims if dim in r)

    def order(self):
        inner = [r for r in subsets(self.dims) if r and self.dims[-1] not in r]
        outer = [r for r in subsets(self.dims) if self.dims[-1] in r]
        return inner + outer

    def finish(self):
        for copy in self.started:
            copy.wait_send()


def add_blocks(target, left, right, extra=None):
    rows = left.shape[0]

    def one(i, carry):
        part = pl.ds(pl.multiple_of(i * 16, 16), 16)
        total = left[part, :].astype(F32) + right[part, :].astype(F32)
        target[part, :] = total.astype(target.dtype)
        return carry

    lax.fori_loop(0, rows // 16, one, 0)


class Scatter:
    def __init__(self, here, dims, first, slot, received, send_sems, recv_sems):
        self.here, self.dims, self.first, self.slot, self.received = here, dims, first, slot, received
        self.send_sems, self.recv_sems = send_sems, recv_sems
        self.started = []

    def number(self, level, r):
        return sum(1 << self.dims[level + 1 :].index(dim) for dim in r)

    def sem(self, level, r):
        below = sum(1 << (len(self.dims) - 1 - i) for i in range(level))
        return below + self.number(level, r)

    def copy(self, level, r):
        dim = self.dims[level]
        source = self.first(self.here.flip(r + dim)) if level == 0 else self.slot(r + dim)
        i = self.sem(level, r)
        return remote(
            source, self.received(level, self.number(level, r)), self.send_sems.at[i], self.recv_sems.at[i], self.here.flip(dim)
        )

    def ordered(self, level):
        rest = self.dims[level + 1 :]
        return sorted(subsets(rest), key=lambda r: [-(dim in r) for dim in rest])

    def send(self, level, r):
        copy = self.copy(level, r)
        copy.start()
        self.started.append(copy)

    def start(self):
        for r in self.ordered(0):
            self.send(0, r)

    def take(self, level, r):
        self.copy(level, r).wait_recv()
        add_blocks(self.slot(r), self.slot(r), self.received(level, self.number(level, r)))
        if level + 1 < len(self.dims) and self.dims[level + 1] in r:
            self.send(level + 1, "".join(dim for dim in r if dim != self.dims[level + 1]))

    def last(self):
        level = len(self.dims) - 1
        self.copy(level, "").wait_recv()
        return self.received(level, 0)

    def steps(self):
        return [(level, r) for level in range(len(self.dims) - 1) for r in self.ordered(level)]

    def finish(self):
        for copy in self.started:
            copy.wait_send()


def dot_nn(left, right):
    return jnp.dot(left, right, preferred_element_type=F32)


def dot_nt(left, right):
    return lax.dot_general(left, right, (((1,), (1,)), ((), ())), preferred_element_type=F32)


def dot_tn(left, right):
    return lax.dot_general(left, right, (((0,), (0,)), ((), ())), preferred_element_type=F32)


def turn(values, cosines, sines):
    return values * cosines + pltpu.roll(values, values.shape[-1] // 2, 1) * sines


def row_scale(values):
    return lax.rsqrt(jnp.mean(values * values, axis=-1, keepdims=True) + EPS)

def forward_kernel(
    tokens, cot, w_query, w_key, w_value, w_out, w_gate, w_up, pack, cosines, sines,
    nf_out, dm_out, gate_out, up_out, packs_out, middle_out, ht_out, wd_out,
    q_out, k_out, v_out, ql_out, kl_out, att_out, den_out,
    ht, normed, weights, partial, got_k, got_y, got_z, got_zz, packs, gain,
    ex_send, ex_recv, w_send, w_recv, fw_send, fw_recv, p_send, p_recv, e_send, e_recv,
    hs, hr, ds, dr, ss, sr, local,
):
    here = my_place()
    x, tp, ctx = here.x, here.tp, here.ctx
    mine = w_gate.shape[0] // 8
    head = cosines.shape[1]
    started, locals_ = [], []

    def local_copy(source, target):
        copy = pltpu.make_async_copy(source, target, local.at[len(locals_)])
        copy.start()
        locals_.append(copy)
        return copy

    greet(here)
    quarter = pl.ds(pl.multiple_of(tp * 16, 16), 16)
    block_rows = pl.ds(pl.multiple_of(x * 16, 16), 16)
    other = here.flip("x")

    exchange_copies = []
    for i, (source, target) in enumerate(((tokens, ht.at[:, here.owner16]), (cot, None))):
        if target is None:
            mine_slot, slot_there = dm_out.at[here.z, :, here.owner8], dm_out.at[other.z, :, other.owner8]
        else:
            mine_slot, slot_there = target, ht.at[:, other.owner16]
        copy = remote(
            source.at[pl.ds(2 * other.x, 2), quarter, :], slot_there.at[:, block_rows, :], ex_send.at[i], ex_recv.at[i], other
        )
        copy.start()
        exchange_copies.append(copy)
        local_copy(source.at[pl.ds(2 * x, 2), quarter, :], mine_slot.at[:, block_rows, :])

    local_copy(pack, packs.at[ctx])
    pack_copies = []
    for step in range(1, 8):
        copy = remote(pack, packs.at[ctx], p_send.at[step], p_recv.at[step], ctx_peer(here, step))
        copy.start()
        pack_copies.append(copy)

    dense = (w_query, w_key, w_value, w_out)
    my_rows = pl.ds(pl.multiple_of(ctx * 256, 256), 256)
    w_copies = {}

    def send_weights(which):
        for j, dims in enumerate(("Z", "z", "Zz")):
            peer = here.flip(dims)
            for i in which:
                copy = remote(
                    dense[i].at[:, pl.ds(pl.multiple_of(peer.z * head, head), head)],
                    weights.at[my_rows, pl.ds(i * head, head)],
                    w_send.at[j, i],
                    w_recv.at[j, i],
                    peer,
                )
                copy.start()
                w_copies[j, i] = copy

    own_weights = [
        local_copy(
            weight.at[:, pl.ds(pl.multiple_of(here.z * head, head), head)], weights.at[my_rows, pl.ds(i * head, head)]
        )
        for i, weight in enumerate(dense)
    ]
    forwards = []

    def pass_weights(j, which):
        place = here.flip(("", "Z", "z", "Zz")[j])
        if j:
            for i in which:
                w_copies[j - 1, i].wait()
        rows = pl.ds(pl.multiple_of(place.ctx * 256, 256), 256)
        columns = pl.ds(which[0] * head, len(which) * head)
        n = 2 * j + (which[0] == 3)
        copy = remote(weights.at[rows, columns], weights.at[rows, columns], fw_send.at[n], fw_recv.at[n], other)
        copy.start()
        forwards.append(copy)

    expert_copies = []

    def send_experts(steps):
        for i, (weight, target) in enumerate(((w_gate, gate_out), (w_up, up_out))):
            for step in steps:
                peer = ctx_peer(here, step)
                copy = remote(
                    weight.at[pl.ds(mine * peer.ctx, mine)],
                    target.at[:, my_rows, :],
                    e_send.at[i, step],
                    e_recv.at[i, step],
                    peer,
                )
                copy.start()
                expert_copies.append(copy)

    for weight, target in ((w_gate, gate_out), (w_up, up_out)):
        local_copy(weight.at[pl.ds(mine * ctx, mine)], target.at[:, my_rows, :])

    heads = [Gather(here, "Zzyk", lambda place, s=s: ht.at[s, place.owner16], hs.at[s], hr.at[s]) for s in range(2)]
    marks = [
        Gather(here, dims, lambda place, s=s: dm_out.at[place.z, s, place.owner8], ds.at[s], dr.at[s])
        for s, dims in ((0, "Zzxyk"), (1, "Zzyxk"))
    ]
    send_weights((0, 1, 2))
    exchange_copies[0].wait()
    locals_[0].wait()
    for gather in heads:
        gather.send("")
    exchange_copies[1].wait()
    locals_[1].wait()
    for gather in marks:
        gather.send("")
    send_weights((3,))
    for copy in own_weights:
        copy.wait()
    pass_weights(0, (0, 1, 2))

    def heads_arrive(*chosen):
        for r in chosen:
            for gather in heads:
                gather.arrive(r)

    def marks_arrive(*chosen):
        for r in chosen:
            for gather in marks:
                gather.arrive(gather.sort(r))

    heads_arrive("Z", "z")
    pass_weights(1, (0, 1, 2))
    pass_weights(2, (0, 1, 2))
    heads_arrive("Zz")
    pass_weights(3, (0, 1, 2))
    marks_arrive("Z", "z", "Zz")
    for j in range(4):
        pass_weights(j, (3,))
    send_experts((2, 4, 6))
    for copy in pack_copies:
        copy.wait()
    locals_[2].wait()
    for i in range(8):
        gain[0:1, i * 256 : (i + 1) * 256] = packs[i, 16:17, :].astype(F32)
        gain[1:2, i * 256 : (i + 1) * 256] = packs[i, 17:18, :].astype(F32)
    qk_gain = jnp.sum(packs[:, 18:20, :head].astype(F32), axis=0)
    packs_out[...] = packs[...]

    def normalise(i, carry):
        rows = ht[i // 16, i % 16].astype(F32)
        target = pl.ds(pl.multiple_of(i * 32, 32), 32)
        normed[target, :] = (rows * row_scale(rows) * gain[0:1, :]).astype(BF16)
        return carry

    heads_arrive("y", "Zy", "zy", "Zzy")
    heads_arrive("k", "Zk", "zk", "Zzk", "yk", "Zyk", "zyk", "Zzyk")
    lax.fori_loop(0, 32, normalise, 0)
    for copy in forwards[:4]:
        copy.wait()
    save_ht = local_copy(ht, ht_out)

    def project(i, carry):
        rows = pl.ds(pl.multiple_of(i * 256, 256), 256)
        table = pl.ds(pl.multiple_of((i % 2) * 256, 256), 256)
        lin = dot_nn(normed[rows, :], weights[:, : 3 * head])
        query_lin, key_lin = lin[:, :head], lin[:, head : 2 * head]
        ql_out[rows, :] = query_lin
        kl_out[rows, :] = key_lin
        v_out[rows, :] = lin[:, 2 * head :].astype(BF16)
        cos, sin = cosines[table, :], sines[table, :]
        q_out[rows, :] = (
            turn(query_lin * row_scale(query_lin) * qk_gain[0:1, :], cos, sin) * head ** (-0.5)
        ).astype(BF16)
        k_out[rows, :] = turn(key_lin * row_scale(key_lin) * qk_gain[1:2, :], cos, sin).astype(BF16)
        return carry

    lax.fori_loop(0, 4, project, 0)
    for copy in forwards[4:]:
        copy.wait()
    send_experts((1, 3, 5, 7))
    save_w = local_copy(weights, wd_out)

    sums = [
        Scatter(
            here,
            "kyzZ",
            lambda place, s=s: partial.at[s, place.owner16],
            lambda r, s=s: partial.at[s, here.flip(r).owner16],
            lambda level, i, s=s: (got_k, got_y, got_z, got_zz)[level].at[s, i],
            ss.at[s],
            sr.at[s],
        )
        for s in range(2)
    ]
    for s in range(2):
        keys = pl.ds(s * 512, 512)

        def attend(i, carry):
            rows = pl.ds(pl.multiple_of(s * 512 + i * 256, 256), 256)
            scores = dot_nt(q_out[rows, :], k_out[keys, :])
            exponent = jnp.exp(scores)
            denominator = jnp.sum(exponent, axis=-1, keepdims=True)
            attended = dot_nn(exponent.astype(BF16), v_out[keys, :]) / denominator
            att_out[rows, :] = attended.astype(BF16)
            den_out[rows, :] = jnp.broadcast_to(denominator, attended.shape)
            attended_low = attended.astype(BF16)

            def column(j, inner):
                columns = pl.ds(pl.multiple_of(j * 512, 512), 512)
                term = dot_nt(attended_low, weights[columns, 3 * head :])
                partial[s, pl.ds(i * 8, 8), :, columns] = term.astype(BF16).reshape(8, 32, 512)
                return inner

            return lax.fori_loop(0, 4, column, carry)

        lax.fori_loop(0, 2, attend, 0)
        sums[s].start()
    def sums_take(level):
        for one in sums:
            for r in one.ordered(level):
                one.take(level, r)

    for r in ("", "Z", "z", "Zz"):
        marks[0].arrive(r + "x")
        marks[1].arrive(r + "y")
    sums_take(0)
    sums_take(1)
    for r in ("", "Z", "z", "Zz"):
        marks[0].arrive(r + "y")
        marks[1].arrive(r + "x")
        marks_arrive(r + "xy")
    sums_take(2)
    for s in range(2):
        rest = sums[s].last()
        total = partial[s, here.owner16].astype(F32) + rest[...].astype(F32)
        middle = ht[s, here.owner16].astype(F32) + total
        middle_out[s] = middle
        nf_out[s] = (middle * row_scale(middle) * gain[1:2, :]).astype(BF16)
    for r in ("k", "xk", "yk", "xyk"):
        marks_arrive(r, "Z" + r, "z" + r, "Zz" + r)
    for copy in expert_copies:
        copy.wait()
    for copy in locals_[7:]:
        copy.wait()
    for part in heads + marks + sums:
        part.finish()


def forward(tokens, cot, w_query, w_key, w_value, w_out, w_gate, w_up, pack, cosines, sines):
    anywhere = pl.BlockSpec(memory_space=pl.ANY)
    vmem = pl.BlockSpec(memory_space=pltpu.VMEM)
    width = tokens.shape[2]
    head = cosines.shape[1]
    mine = w_gate.shape[0] // 8
    hidden = w_gate.shape[2]
    all_rows = jax.ShapeDtypeStruct((4, 2, 8, 32, width), BF16)
    weight = jax.ShapeDtypeStruct((mine, width, hidden), BF16)
    low, high = jax.ShapeDtypeStruct((1024, head), BF16), jax.ShapeDtypeStruct((1024, head), F32)
    dma = pltpu.SemaphoreType.DMA
    return pl.pallas_call(
        forward_kernel,
        out_shape=(
            jax.ShapeDtypeStruct((2, 32, width), BF16), all_rows, weight, weight,
            jax.ShapeDtypeStruct((8,) + pack.shape, BF16),
            jax.ShapeDtypeStruct((2, 32, width), F32),
            jax.ShapeDtypeStruct((2, 16, 32, width), BF16),
            jax.ShapeDtypeStruct((width, 4 * head), BF16),
            low, low, low, high, high, low, high,
        ),
        in_specs=[anywhere] * 9 + [vmem] * 2,
        out_specs=(vmem,) + (anywhere,) * 3 + (vmem, vmem) + (anywhere,) * 2 + (vmem,) * 7,
        scratch_shapes=[
            pltpu.VMEM((2, 16, 32, width), BF16),
            pltpu.VMEM((1024, width), BF16),
            pltpu.VMEM((width, 4 * head), BF16),
            pltpu.VMEM((2, 16, 32, width), BF16),
            pltpu.VMEM((2, 8, 32, width), BF16),
            pltpu.VMEM((2, 4, 32, width), BF16),
            pltpu.VMEM((2, 2, 32, width), BF16),
            pltpu.VMEM((2, 1, 32, width), BF16),
            pltpu.VMEM((8,) + pack.shape, BF16),
            pltpu.VMEM((8, width), F32),
            dma((2,)), dma((2,)), dma((3, 4)), dma((3, 4)), dma((8,)), dma((8,)), dma((8,)), dma((8,)),
            dma((3, 8)), dma((3, 8)), dma((2, 16)), dma((2, 16)), dma((2, 32)), dma((2, 32)),
            dma((2, 16)), dma((2, 16)), dma((16,)),
        ],
        compiler_params=pltpu.CompilerParams(collective_id=0, has_side_effects=True, vmem_limit_bytes=VMEM_LIMIT),
        cost_estimate=pl.CostEstimate(flops=4 * 10**9, bytes_accessed=64 * 10**6, transcendentals=10**6),
    )(tokens, cot, w_query, w_key, w_value, w_out, w_gate, w_up, pack, cosines, sines)

def norm_gradient(gradient, values, scale, gain):
    weighted = gradient * gain
    return scale * weighted - values * (scale * scale * scale * jnp.mean(weighted * values, axis=-1, keepdims=True))


Z_PARTS = ("", "Zz", "z", "Z")
Z_ORDER = ("Zz", "z", "Z", "")


def later_kernel(
    nf_own, dm_in, gate_in, up_in, down_in, packs, chosen, middle, ht_in, wd_in,
    q_in, k_in, v_in, ql_in, kl_in, att_in, den_in, cosines, sines,
    layer_out, input_grad, gate_out, up_out, down_out, dense_out, mixed_out, small_out,
    nf, dm, part, w_gate, w_up, w_down, grad_down, hidden, active, grad_gate, grad_up, grad_logits, router, stage,
    got_k, got_a, got_b, got_z, got_zz, gain, grad_middle, lin_t, key_sum, value_sum, scales, columns_sum, qk_sum, sg, sg_k, sg_y, sg_all,
    ns, nr, rs, rr, e_send, e_recv, hs, hr, ms, mr, ss, sr, o_send, o_recv, o2_send, o2_recv, d_send, d_recv, g_send, g_recv,
    local, stage_sem, ready,
):
    here = my_place()
    x, tp, ctx = here.x, here.tp, here.ctx
    other = here.flip("x")
    width = nf.shape[4]
    head = cosines.shape[1]
    experts = packs.shape[1] - 32
    mine = w_gate.shape[0]
    locals_ = []

    def local_copy(source, target):
        copy = pltpu.make_async_copy(source, target, local.at[len(locals_)])
        copy.start()
        locals_.append(copy)
        return copy

    own_copy = local_copy(nf_own, nf.at[here.z, :, here.owner8])
    loads = [local_copy(gate_in, w_gate), local_copy(up_in, w_up), local_copy(chosen, grad_logits)]
    dm_load = local_copy(dm_in, dm)
    greet(here)
    gathers = [
        Gather(here, dims, lambda place, s=s: nf.at[place.z, s, place.owner8], ns.at[s], nr.at[s], nf_own.at[s])
        for s, dims in ((0, "Zzxyk"), (1, "Zzyxk"))
    ]
    for gather in gathers:
        gather.send("")
    quarter = pl.ds(pl.multiple_of(tp * 16, 16), 16)
    block_rows = pl.ds(pl.multiple_of(x * 16, 16), 16)
    other_rows = pl.ds(pl.multiple_of(other.x * 16, 16), 16)
    my_rows = pl.ds(pl.multiple_of(ctx * 256, 256), 256)
    down_copies = [local_copy(down_in.at[pl.ds(mine * ctx, mine)], w_down.at[:, my_rows, :])]

    def send_down(steps):
        for step in steps:
            peer = ctx_peer(here, step)
            copy = remote(
                down_in.at[pl.ds(mine * peer.ctx, mine)], w_down.at[:, my_rows, :], e_send.at[0, step], e_recv.at[0, step], peer
            )
            copy.start()
            down_copies.append(copy)

    router[...] = jnp.zeros_like(router)
    for i in range(8):
        columns = slice(i * 256, (i + 1) * 256)
        router[0:experts, columns] = packs[i, 0:experts, :]
        gain[0:1, columns] = packs[i, 16:17, :].astype(F32)
        gain[1:2, columns] = packs[i, 17:18, :].astype(F32)
    qk_gain = jnp.sum(packs[:, 18:20, :head].astype(F32), axis=0)

    def arrive(s, *chosen_ones):
        for r in chosen_ones:
            gathers[s].arrive(gathers[s].sort(r))

    parts = [
        Scatter(
            here,
            dims,
            lambda place, s=s: part.at[place.z, s, place.owner8],
            lambda r, s=s: part.at[here.flip(r).z, s, here.flip(r).owner8],
            lambda level, i, s=s: (got_k, got_a, got_b, got_z, got_zz)[level].at[s, i],
            rs.at[s],
            rr.at[s],
        )
        for s, dims in enumerate(ALL_ORDERS)
    ]

    def in_part(s, level, z_part):
        inner = parts[s].dims[level + 1 : 3]
        return [r for r in parts[s].ordered(level) if set(r) == (set(r) & set(inner)) | set(z_part)]

    def take(level, z_part):
        for s in range(2):
            for r in in_part(s, level, z_part):
                parts[s].take(level, r)

    lanes = lax.broadcasted_iota(jnp.int32, (256, 128), 1)

    def weights_of(rows):
        logits = jnp.where(lanes < experts, dot_nt(rows, router[...]), -1e30)
        expo = jnp.exp(logits - jnp.max(logits, axis=-1, keepdims=True))
        return expo / jnp.sum(expo, axis=-1, keepdims=True)

    def first_pass(z, s):
        flat = pl.ds(pl.multiple_of(z * 512 + s * 256, 256), 256)
        rows = nf[z, s].reshape(256, width)
        probs = weights_of(rows)
        picked = probs * grad_logits[flat, :].astype(F32)
        for e in range(mine):
            gate = jnp.sum(picked * (lanes == here.ctx * mine + e).astype(F32), axis=-1, keepdims=True)
            gate_pre, up_pre = dot_nn(rows, w_gate[e]), dot_nn(rows, w_up[e])
            sigmoid_gate = jax.nn.sigmoid(gate_pre)
            silu_gate = gate_pre * sigmoid_gate
            activated = silu_gate * up_pre
            hidden[e, flat, :] = (gate * activated).astype(BF16)
            active[e, flat, :] = activated.astype(BF16)
            grad_up[e, flat, :] = silu_gate.astype(BF16)
            grad_gate[e, flat, :] = (up_pre * sigmoid_gate * (1.0 + gate_pre * (1.0 - sigmoid_gate))).astype(BF16)

    def second_pass(z, s):
        flat = pl.ds(pl.multiple_of(z * 512 + s * 256, 256), 256)
        grad_rows = dm[z, s].reshape(256, width)
        probs = weights_of(nf[z, s].reshape(256, width))
        picked = grad_logits[flat, :].astype(F32)
        placed = jnp.zeros((256, 128), F32)
        for e in range(mine):
            this = (lanes == here.ctx * mine + e).astype(F32)
            named = jnp.sum(picked * this, axis=-1, keepdims=True)
            gate = jnp.sum(probs * this, axis=-1, keepdims=True) * named
            grad_hidden = dot_nn(grad_rows, w_down[e])
            dot = jnp.sum(grad_hidden * active[e, flat, :].astype(F32), axis=-1, keepdims=True)
            placed = placed + dot * named * this
            grad_act = gate * grad_hidden
            grad_up[e, flat, :] = (grad_act * grad_up[e, flat, :].astype(F32)).astype(BF16)
            grad_gate[e, flat, :] = (grad_act * grad_gate[e, flat, :].astype(F32)).astype(BF16)
        share = (probs * (placed - jnp.sum(probs * placed, axis=-1, keepdims=True))).astype(BF16)
        grad_logits[flat, :] = share

        def column(j, carry):
            columns = pl.ds(pl.multiple_of(j * 512, 512), 512)
            term = dot_nn(share, router[:, columns])
            mixed = jnp.zeros((256, 512), F32)
            for e in range(mine):
                mixed = mixed + dot_nt(hidden[e, flat, :], w_down[e, columns, :])
                term = term + dot_nt(grad_gate[e, flat, :], w_gate[e, columns, :])
                term = term + dot_nt(grad_up[e, flat, :], w_up[e, columns, :])
            stage[s, :, :, columns] = mixed.astype(BF16).reshape(8, 32, 512)
            part[z, s, :, :, columns] = term.astype(BF16).reshape(8, 32, 512)
            return carry

        lax.fori_loop(0, width // 512, column, 0)

    for number, z_part in enumerate(Z_PARTS):
        if number == 0:
            arrive(0, "x")
            arrive(1, "y")
            for s in range(2):
                arrive(s, "Z", "z")
            arrive(0, "y", "xy")
            arrive(1, "x", "xy")
            for s in range(2):
                arrive(s, "Zz")
            send_down((2, 4, 6))
            for r in ("k", "xk", "yk", "xyk"):
                for s in range(2):
                    arrive(s, r)
            own_copy.wait()
            for copy in loads:
                copy.wait()
        else:
            if number == 1:
                for z_other in Z_PARTS[1:]:
                    arrive(0, z_other + "x")
                    arrive(1, z_other + "y")
                send_down((1, 3, 5, 7))
            for inner in ("x", "y", "xy", "k", "xk", "yk", "xyk"):
                for s in range(2):
                    if inner != ("x", "y")[s]:
                        arrive(s, z_part + inner)
        z = here.flip(z_part).z

        def both(s, carry):
            first_pass(z, s)
            return carry

        lax.fori_loop(0, 2, both, 0)
    dm_load.wait()
    def weigh_down(i, carry):
        columns = pl.ds(pl.multiple_of(i * 256, 256), 256)
        grad_rows = dm[:, :, :, :, columns].reshape(2048, 256)
        for e in range(mine):
            grad_down[e, columns, :] = dot_tn(grad_rows, hidden[e]).astype(BF16)
        return carry

    lax.fori_loop(0, 8, weigh_down, 0)
    for copy in down_copies:
        copy.wait()
    give_copies = [local_copy(grad_down.at[:, my_rows, :], down_out.at[pl.ds(mine * ctx, mine)])]
    queue = [(1, grad_down, down_out, step) for step in (2, 4, 6, 1, 3, 5, 7)]
    for step in (2, 4, 6, 1, 3, 5, 7):
        queue += [(2, w_gate, gate_out, step), (3, w_up, up_out, step)]

    def give(count):
        for which, source, target, step in queue[:count]:
            peer = ctx_peer(here, step)
            rows = pl.ds(pl.multiple_of(peer.ctx * 256, 256), 256)
            copy = remote(
                source.at[:, rows, :], target.at[pl.ds(mine * ctx, mine)], e_send.at[which, step], e_recv.at[which, step], peer
            )
            copy.start()
            give_copies.append(copy)
        del queue[:count]

    give(3)
    stage_copy = None
    for number, z_part in enumerate(Z_ORDER):
        z = here.flip(z_part).z
        if stage_copy is not None:
            stage_copy.wait()

        def both_again(s, carry):
            second_pass(z, s)
            return carry

        lax.fori_loop(0, 2, both_again, 0)
        stage_copy = pltpu.make_async_copy(stage, mixed_out.at[z], stage_sem.at[0])
        stage_copy.start()
        for s in range(2):
            for r in in_part(s, 0, z_part):
                parts[s].send(0, r)
        if number >= 1:
            take(0, Z_ORDER[number - 1])
        if number >= 2:
            take(1, Z_ORDER[number - 2])
        if number >= 3:
            take(2, Z_ORDER[number - 3])
        if number >= 1:
            give(1)

    def weigh(step):
        i = (ctx + step) % 8
        columns = pl.ds(pl.multiple_of(i * 256, 256), 256)
        rows = nf[:, :, :, :, columns].reshape(2048, 256)
        for e in range(mine):
            w_gate[e, columns, :] = dot_tn(rows, grad_gate[e]).astype(BF16)
            w_up[e, columns, :] = dot_tn(rows, grad_up[e]).astype(BF16)
        sg[i, 0:16, :] = dot_tn(grad_logits[...], rows)[0:16, :]

    def weigh_some(start, stop, stride, offset):
        def one(n, carry):
            weigh(n * stride + offset)
            return carry

        lax.fori_loop(start, stop, one, 0)

    weigh_some(1, 2, 2, 0)
    take(0, Z_ORDER[3])
    take(1, Z_ORDER[2])
    take(2, Z_ORDER[1])
    weigh_some(2, 4, 2, 0)
    take(1, Z_ORDER[3])
    take(2, Z_ORDER[2])
    for s in range(2):
        parts[s].take(3, "Z")
    weigh_some(0, 3, 2, 1)
    take(2, Z_ORDER[3])
    for s in range(2):
        parts[s].take(3, "")
    weigh_some(3, 4, 2, 1)
    weigh_some(0, 1, 2, 0)
    give(1)
    stage_copy.wait()
    for one in gathers:
        one.finish()
    for s in range(2):
        stage[s, 0] = dm[here.z, s, here.owner8]
    load_w = [local_copy(wd_in.at[:, pl.ds(n * 256, 256)], w_down.at[n]) for n in range(2)]
    load_ht = local_copy(ht_in, nf.at[pl.ds(0, 2)])
    load_w += [local_copy(q_in, grad_logits.at[pl.ds(0, 1024)]), local_copy(k_in, grad_logits.at[pl.ds(1024, 1024)])]
    for peer in everyone(here):
        pl.semaphore_signal(ready, inc=1, device_id=peer.device, device_id_type=MESH_ID)

    own8, own_half = here.owner16 % 8, here.owner16 // 8
    mixed, loads = [], []
    for s, dims in enumerate(ALL_ORDERS):

        def index(r, dims=dims):
            return sum(1 << dims[1:].index(dim) for dim in r)

        def landing(level, i, s=s):
            if level == 0:
                return nf.at[2 + s, i // 8, i % 8]
            return got_k.at[s, (0, 0, 8, 12, 14)[level] + i]

        mixed.append(
            Scatter(
                here,
                dims,
                lambda place, s=s: mixed_out.at[place.z, s, place.owner8],
                lambda r, s=s, index=index: dm.at[2 + s, index(r) // 8, index(r) % 8],
                landing,
                ms.at[s],
                mr.at[s],
            )
        )
        for r in mixed[s].ordered(0):
            there = here.flip(r)
            loads.append(local_copy(mixed_out.at[there.z, s, there.owner8], mixed[s].slot(r)))

    def mixed_take(level, which=(0, 1)):
        for s in which:
            for r in mixed[s].ordered(level):
                mixed[s].take(level, r)

    columns_sum[...] = jnp.zeros_like(columns_sum)
    for s in range(2):
        gradient = part[here.z, s, here.owner8].astype(F32) + parts[s].last()[...].astype(F32)
        values = middle[s]
        scale = row_scale(values)
        columns_sum[1:2, :] += jnp.sum(gradient * values * scale, axis=0, keepdims=True)
        total = stage[s, 0].astype(F32) + norm_gradient(gradient, values, scale, gain[1:2, :])
        grad_middle[s] = total
        stage[s, 1] = total.astype(BF16)
    heads = [
        Gather(
            here, "Zzyk", lambda place, s=s: dm.at[s, place.owner16 // 8, place.owner16 % 8], hs.at[s], hr.at[s], stage.at[s, 1]
        )
        for s in range(2)
    ]
    for one in parts:
        one.finish()
    pl.semaphore_wait(ready, len(everyone(here)))
    for gather in heads:
        gather.send("")
    own_copy = local_copy(stage.at[:, 1], dm.at[pl.ds(0, 2), own_half, own8])
    for one in mixed:
        one.start()
    give_copies.append(local_copy(w_gate.at[:, my_rows, :], gate_out.at[pl.ds(mine * ctx, mine)]))
    give_copies.append(local_copy(w_up.at[:, my_rows, :], up_out.at[pl.ds(mine * ctx, mine)]))
    for r in ("Z", "z", "Zz"):
        for gather in heads:
            gather.arrive(r)
    give(3)
    load_ht.wait()

    def normalise(i, carry):
        s, a, c = i // 16, (i % 16) // 8, i % 8
        rows = nf[s, a, c].astype(F32)
        scale = row_scale(rows)
        scales[pl.ds(pl.multiple_of(i * 32, 32), 32), :] = jnp.broadcast_to(scale, (32, head))
        part[2 + s, a, c] = (rows * scale * gain[0:1, :]).astype(BF16)
        return carry

    lax.fori_loop(0, 32, normalise, 0)
    give(1)
    for copy in loads:
        copy.wait()
    mixed_take(0, (1,))
    for r in heads[0].order():
        if r not in ("Z", "z", "Zz"):
            for gather in heads:
                gather.arrive(r)
    own_copy.wait()
    for copy in load_w:
        copy.wait()

    give(2)
    qk_sum[...] = jnp.zeros_like(qk_sum)
    score_scale = head ** (-0.5)
    for s in range(2):
        all_rows = pl.ds(s * 512, 512)
        upper_rows = pl.ds(1024 + s * 512, 512)
        key_sum[...] = jnp.zeros_like(key_sum)
        value_sum[...] = jnp.zeros_like(value_sum)

        def attend(i, carry):
            rows = pl.ds(pl.multiple_of(s * 512 + i * 256, 256), 256)
            upper = pl.ds(pl.multiple_of(1024 + s * 512 + i * 256, 256), 256)
            table = pl.ds(pl.multiple_of(i * 256, 256), 256)
            gradient = dot_nn(dm[s, i].reshape(256, width), w_down[1, :, head:])
            attended, denominator = att_in[rows, :].astype(F32), den_in[rows, :]
            active[0, upper, head:] = att_in[rows, :]
            exponent = jnp.exp(dot_nt(grad_logits[rows, :], grad_logits[upper_rows, :]))
            grad_acc = (gradient / denominator).astype(BF16)
            grad_total = -jnp.sum(gradient * attended, axis=-1, keepdims=True) / denominator[:, :1]
            grad_prob = dot_nt(grad_acc, v_in[all_rows, :])
            grad_score = (exponent * (grad_prob + grad_total)).astype(BF16)
            grad_query = dot_nn(grad_score, grad_logits[upper_rows, :]) * score_scale
            key_sum[...] += dot_tn(grad_score, grad_logits[rows, :])
            value_sum[...] += dot_tn(exponent.astype(BF16), grad_acc)
            grad_query = turn(grad_query, cosines[table, :], -sines[table, :])
            values = ql_in[rows, :]
            scale = row_scale(values)
            qk_sum[0:1, :] += jnp.sum(grad_query * values * scale, axis=0, keepdims=True)
            active[0, rows, :head] = norm_gradient(grad_query, values, scale, qk_gain[0:1, :]).astype(BF16)
            return carry

        lax.fori_loop(0, 2, attend, 0)
        grad_keys = turn(key_sum[...], cosines[...], -sines[...])
        values = kl_in[all_rows, :]
        scale = row_scale(values)
        qk_sum[1:2, :] += jnp.sum(grad_keys * values * scale, axis=0, keepdims=True)
        active[0, all_rows, head:] = norm_gradient(grad_keys, values, scale, qk_gain[1:2, :]).astype(BF16)
        active[0, upper_rows, :head] = value_sum[...].astype(BF16)

    give(1)
    sums = [
        Scatter(
            here,
            "kyzZ",
            lambda place, s=s: part.at[s, place.owner16 // 8, place.owner16 % 8],
            lambda r, s=s: part.at[s, here.flip(r).owner16 // 8, here.flip(r).owner16 % 8],
            lambda level, i, s=s: (got_a, got_b, got_z, got_zz)[level].at[s, i],
            ss.at[s],
            sr.at[s],
        )
        for s in range(2)
    ]
    for s in range(2):

        def project(n, carry):
            i, j = n // 4, n % 4
            rows = pl.ds(pl.multiple_of(s * 512 + i * 256, 256), 256)
            upper = pl.ds(pl.multiple_of(1024 + s * 512 + i * 256, 256), 256)
            columns = pl.ds(pl.multiple_of(j * 512, 512), 512)
            term = dot_nt(active[0, rows, :], w_down[0, columns, :])
            term = term + dot_nt(active[0, upper, :head], w_down[1, columns, :head])
            unit = nf[s, i, :, :, columns].reshape(256, 512).astype(F32) * scales[rows, :1]
            columns_sum[0:1, columns] += jnp.sum(term * unit, axis=0, keepdims=True)
            part[s, i, :, :, columns] = term.astype(BF16).reshape(8, 32, 512)
            return carry

        lax.fori_loop(0, 8, project, 0)
        sums[s].start()

    give(1)
    for one in sums:
        for r in one.ordered(0):
            one.take(0, r)

    def slot(i):
        return hidden.at[i // 4, pl.ds(pl.multiple_of((i % 4) * 512, 512), 512), :]

    for i in range(4):
        rows, upper = slice(i * 256, (i + 1) * 256), slice(1024 + i * 256, 1280 + i * 256)
        lin_t[0 : 2 * head, rows] = active[0, rows, :].T
        lin_t[2 * head :, rows] = active[0, upper, :].T

    def weigh_dense(i, carry):
        columns = pl.ds(pl.multiple_of(i * 256, 256), 256)
        start = (i % 4) * 512
        rows = part[2:4, :, :, :, columns].reshape(1024, 256)
        term = dot_nn(lin_t[: 3 * head, :], rows).astype(BF16)
        hidden[i // 4, pl.ds(pl.multiple_of(start, 128), 3 * head), :] = term
        return carry

    def weigh_out(i, carry):
        columns = pl.ds(pl.multiple_of(i * 256, 256), 256)
        start = (i % 4) * 512 + 3 * head
        rows = dm[0:2, :, :, :, columns].reshape(1024, 256)
        term = dot_nn(lin_t[3 * head :, :], rows).astype(BF16)
        hidden[i // 4, pl.ds(pl.multiple_of(start, 128), head), :] = term
        return carry

    lax.fori_loop(0, 8, weigh_dense, 0)
    lax.fori_loop(0, 8, weigh_out, 0)

    def across(n):
        return grad_gate.at[0, pl.ds(n * 512, 512), :]

    def along(n):
        return grad_gate.at[1, pl.ds(n * 512, 512), :]

    dense_copies = []
    for i, dims in enumerate(("", "Z", "z", "Zz")):
        copy = remote(slot(other.flip(dims).ctx), across(i), d_send.at[i], d_recv.at[i], other)
        copy.start()
        dense_copies.append(copy)

    for i in range(8):
        columns = slice(i * 256, (i + 1) * 256)
        sg[i, 16:18, :] = columns_sum[0:2, columns]
        sg[i, 18:20, :head] = qk_sum[0:2, :]
        sg[i, 18:20, head:] = jnp.zeros((2, 256 - head), F32)
        sg[i, 20:24, :] = jnp.zeros((4, 256), F32)
    sg_copies = [remote(sg, sg_k, g_send.at[0], g_recv.at[0], here.flip("k"))]
    sg_copies[0].start()
    give(2)
    for one in sums:
        for r in one.ordered(1):
            one.take(1, r)
    sg_copies[0].wait()
    sg[...] = sg[...] + sg_k[...]
    sg_copies.append(remote(sg, sg_y, g_send.at[8], g_recv.at[8], here.flip("y")))
    sg_copies[1].start()
    mixed_take(0, (0,))
    mixed_take(1, (1,))
    for one in sums:
        for r in one.ordered(2):
            one.take(2, r)
    for s in range(2):
        gradient = part[s, own_half, own8].astype(F32) + sums[s].last()[...].astype(F32)
        values = nf[s, own_half, own8].astype(F32)
        total = grad_middle[s] + norm_gradient(gradient, values, row_scale(values), gain[0:1, :])
        stage[s, 3] = total.astype(BF16)

    hands, hand_locals = [], []

    def hand_out(owned, target, sends, receives):
        cross = remote(
            owned.at[:, other_rows, :], target.at[pl.ds(2 * x, 2), quarter, :], sends.at[2, 0], receives.at[2, 0], other
        )
        cross.start()
        parts = [
            Gather(
                here,
                "yk",
                lambda place, which=which: target.at[
                    pl.ds(2 * which, 2), pl.ds(pl.multiple_of(place.tp * 16, 16), 16), :
                ],
                sends.at[i],
                receives.at[i],
                own,
            )
            for i, (which, own) in enumerate(((x, owned.at[:, block_rows, :]), (other.x, None)))
        ]
        parts[0].send("")
        hand_locals.append(local_copy(owned.at[:, block_rows, :], target.at[pl.ds(2 * x, 2), quarter, :]))
        hands.append((cross, parts))

    def hand_on(cross, parts):
        cross.wait()
        parts[1].send("")
        for r in parts[0].order():
            for part in parts:
                part.arrive(r)
        for part in parts:
            part.finish()

    hand_out(stage.at[:, 3], input_grad, o_send, o_recv)
    give(1)
    sg_copies[1].wait()
    sg[...] = sg[...] + sg_y[...]
    for step in range(1, 8):
        peer = ctx_peer(here, step)
        copy = remote(sg.at[peer.ctx], sg_all.at[ctx], g_send.at[step], g_recv.at[step], peer)
        copy.start()
        sg_copies.append(copy)
    for copy in dense_copies:
        copy.wait()
    z_copies = []
    for i, dims in enumerate(("Z", "z", "Zz", "")):
        place = here.flip(dims)
        add_blocks(slot(place.ctx), slot(place.ctx), across(("", "Z", "z", "Zz").index(dims)))
        if dims:
            copy = remote(slot(place.ctx), along(i), d_send.at[4 + i], d_recv.at[4 + i], place)
            copy.start()
            z_copies.append((dims, copy))
    mixed_take(1, (0,))
    mixed_take(2)
    hand_on(*hands[0])
    mixed_take(3)
    give(len(queue))
    for s in range(2):
        total = dm[2 + s, 0, 0].astype(F32) + mixed[s].last()[...].astype(F32)
        stage[s, 2] = (middle[s] + total).astype(BF16)
    hand_out(stage.at[:, 2], layer_out, o2_send, o2_recv)
    saves = [local_copy(slot(ctx), dense_out.at[here.z])]
    for i, (dims, copy) in enumerate(z_copies):
        copy.wait()
        saves.append(local_copy(along(i), dense_out.at[here.flip(dims).z]))
    for copy in sg_copies[2:]:
        copy.wait()
    sg_all[ctx] = sg[ctx]
    small_out[...] = jnp.sum(sg_all[...], axis=0)
    hand_on(*hands[1])
    for copy in give_copies + hand_locals + saves:
        copy.wait()
    for one in heads + mixed + sums:
        one.finish()


def later(*arrays):
    nf_own, dm, gate_w, up_w, raw_down = arrays[:5]
    anywhere = pl.BlockSpec(memory_space=pl.ANY)
    vmem = pl.BlockSpec(memory_space=pltpu.VMEM)
    width, head = nf_own.shape[2], arrays[10].shape[1]
    mine, _, units = gate_w.shape
    dma = pltpu.SemaphoreType.DMA
    all_rows = (4, 2, 8, 32, width)
    tokens = jax.ShapeDtypeStruct((4, 64, width), BF16)
    expert = jax.ShapeDtypeStruct(raw_down.shape, BF16)
    return pl.pallas_call(
        later_kernel,
        out_shape=(
            tokens, tokens, expert, expert, expert,
            jax.ShapeDtypeStruct((4, 4 * head, 256), BF16),
            jax.ShapeDtypeStruct(all_rows, BF16),
            jax.ShapeDtypeStruct((24, 256), F32),
        ),
        in_specs=[anywhere] * 5 + [vmem, anywhere, vmem] + [anywhere] * 4 + [vmem] * 7,
        out_specs=(anywhere,) * 7 + (vmem,),
        scratch_shapes=[
            *[pltpu.VMEM(all_rows, BF16) for _ in range(3)],
            *[pltpu.VMEM(gate_w.shape, BF16) for _ in range(4)],
            *[pltpu.VMEM((mine, 2048, units), BF16) for _ in range(4)],
            pltpu.VMEM((2048, 128), BF16),
            pltpu.VMEM((128, width), BF16),
            pltpu.VMEM((2, 8, 32, width), BF16),
            *[pltpu.VMEM((2, n, 32, width), BF16) for n in (16, 8, 4, 2, 1)],
            pltpu.VMEM((8, width), F32),
            pltpu.VMEM((2, 32, width), F32),
            pltpu.VMEM((4 * head, 1024), BF16),
            pltpu.VMEM((512, head), F32),
            pltpu.VMEM((512, head), F32),
            pltpu.VMEM((1024, head), F32),
            pltpu.VMEM((8, width), F32),
            pltpu.VMEM((8, head), F32),
            *[pltpu.VMEM((8, 24, 256), F32) for _ in range(4)],
            dma((2, 32)), dma((2, 32)), dma((2, 32)), dma((2, 32)), dma((4, 8)), dma((4, 8)), dma((2, 16)), dma((2, 16)),
            dma((2, 32)), dma((2, 32)), dma((2, 16)), dma((2, 16)), dma((3, 4)), dma((3, 4)), dma((3, 4)), dma((3, 4)),
            dma((8,)), dma((8,)), dma((9,)), dma((9,)), dma((64,)), dma((1,)), pltpu.SemaphoreType.REGULAR,
        ],
        compiler_params=pltpu.CompilerParams(
            collective_id=1, has_side_effects=True, vmem_limit_bytes=VMEM_LIMIT
        ),
        cost_estimate=pl.CostEstimate(flops=48 * 10**9, bytes_accessed=64 * 10**6, transcendentals=10**6),
    )(*arrays)

ALL_ORDERS = ("kyxzZ", "kxyzZ")


def per_device_fast(
    tokens, cotangent, routes, attn_gain, ffn_gain, qk_gain, w_query, w_key, w_value, w_out, router, w_gate, w_up, w_down
):
    width = tokens.shape[2]
    head_size = qk_gain.shape[0] * 8
    half_size = head_size // 2
    experts = w_gate.shape[0]
    mine = experts // 8
    hidden_units = w_gate.shape[2]
    ctx, tp = lax.axis_index("ctx"), lax.axis_index("tp")
    z, x = ctx // 2, ctx % 2
    f32, bf16 = F32, BF16

    chosen = jnp.sum((routes[..., None] == jnp.arange(experts)).astype(bf16), axis=2)
    spots = (jnp.arange(head_size)[None, :] == (ctx * 16 + jnp.arange(16))[:, None]).astype(bf16)
    qk_rows = jnp.einsum("gc,gh->ch", qk_gain, spots, preferred_element_type=f32).astype(bf16)
    columns = jnp.concatenate(
        [router, attn_gain[:, None], ffn_gain[:, None], jnp.zeros((256, 14), bf16), chosen.reshape(-1, experts)], axis=1
    )
    pack = columns.T + jnp.pad(qk_rows, ((18, 28), (0, 256 - head_size)))

    zs, ys, ks, bs, i = np.meshgrid(np.arange(4), np.arange(2), np.arange(2), np.arange(2), np.arange(16), indexing="ij")
    positions = ((zs * 2 + bs) * 64 + (ys * 2 + ks) * 16 + i).reshape(-1).astype(np.float32)
    exponents = np.float32(-2.0) * np.arange(half_size).astype(np.float32) / np.float32(head_size)
    angles = positions[:, None] * (np.float32(ROPE_BASE) ** exponents)[None, :]
    cosines = jnp.asarray(np.tile(np.cos(angles), (1, 2)))
    sines = jnp.asarray(np.concatenate([-np.sin(angles), np.sin(angles)], axis=1))

    (
        nf, dm, gate_w, up_w, packs, middle, head_tokens, dense, query, keys, value_rows, query_lin, key_lin, attended, denominator,
    ) = forward(tokens, cotangent, w_query, w_key, w_value, w_out, w_gate, w_up, pack, cosines, sines)

    chosen = packs[:, 32:48].reshape(4, 2, experts, 2, 2, 4, 16)
    chosen = jnp.transpose(chosen, (0, 4, 3, 5, 1, 6, 2)).reshape(-1, experts)
    chosen = jnp.pad(chosen, ((0, 0), (0, 128 - experts)))
    layer_out, input_grad, grad_gate_w, grad_up_w, grad_down_w, dense_grad, _, small = later(
        nf, dm, gate_w, up_w, w_down, packs, chosen, middle, head_tokens.reshape(2, 2, 8, 32, width), dense,
        query, keys, value_rows, query_lin, key_lin, attended, denominator, cosines, sines,
    )
    dense_grad = jnp.transpose(dense_grad.astype(f32).reshape(4, 4, head_size, 256), (1, 3, 0, 2)).reshape(4, 256, 4 * head_size)
    return (
        layer_out,
        input_grad,
        small[16],
        small[17],
        lax.dynamic_slice_in_dim(small[18:20], ctx * 16, 16, 1).T,
        dense_grad[0],
        dense_grad[1],
        dense_grad[2],
        dense_grad[3],
        small[:experts].T,
        grad_gate_w.astype(f32),
        grad_up_w.astype(f32),
        grad_down_w.astype(f32),
    )


def solution(mesh):
    fast = mesh.shape["ctx"] == 8 and mesh.shape["tp"] == 4
    return jax.shard_map(
        per_device_fast if fast else per_device,
        mesh=mesh,
        in_specs=(
            P(None, "ctx", None),
            P(None, "ctx", None),
            P(None, "ctx", None),
            P("ctx"),
            P("ctx"),
            P("ctx", None),
            P("ctx", "tp"),
            P("ctx", "tp"),
            P("ctx", "tp"),
            P("ctx", "tp"),
            P("ctx", None),
            P(None, "ctx", "tp"),
            P(None, "ctx", "tp"),
            P(None, "ctx", "tp"),
        ),
        out_specs=(
            P(None, "ctx", None),
            P(None, "ctx", None),
            P("ctx"),
            P("ctx"),
            P("ctx", None),
            P("ctx", "tp"),
            P("ctx", "tp"),
            P("ctx", "tp"),
            P("ctx", "tp"),
            P("ctx", None),
            P(None, "ctx", "tp"),
            P(None, "ctx", "tp"),
            P(None, "ctx", "tp"),
        ),
        check_vma=False,
    )
```
